32 devices in a mesh: dp: 8 (over z, x), mp: 4 (over y, core).
Axes of the slice: x: 2, y: 2, z: 4, core: 2. Of those that a mesh axis runs over, the one named last changes fastest.
Arguments:
- token_ids: int32 [16, 512], P('dp'), may hold values from 0 to 42111
- seg_lengths: int32 [16, 4], P('dp'), may hold values from 1 to 256, 512 in all within a row
- counted: int32 [16, 512], P('dp'), may hold values from 0 to 1
- unit_slot: int32 [248], replicated, may hold values from 0 to 335, as said below
- master: float32 [336, 224, 1120], P('dp', 'mp'), may hold values from -1.07570575 to 1.07570575
- first_moment: float32 [336, 224, 1120], P('dp', 'mp'), may hold values from -8.443361e-05 to 8.443361e-05
- second_moment: float32 [336, 224, 1120], P('dp', 'mp'), may hold values from 8.4541124e-10 to 3.375216e-09
- norm_params: float32 [6, 1120], replicated, may hold values from -2 to 2
- norm_first: float32 [6, 1120], replicated, may hold values from -0.00068459683 to 0.00068459683
- norm_second: float32 [6, 1120], replicated, may hold values from 5.4646353e-08 to 2.1537093e-07
Outputs:
- new_master: float32 [336, 224, 1120], P('dp', 'mp')
- new_first: float32 [336, 224, 1120], P('dp', 'mp')
- new_second: float32 [336, 224, 1120], P('dp', 'mp')
- new_norms: float32 [6, 1120], replicated
- new_norm_first: float32 [6, 1120], replicated
- new_norm_second: float32 [6, 1120], replicated
- clip_norm: float32 [], replicated
- loss_sum: float32 [], replicated
- loss_count: float32 [], replicated
The draws below stay inside these ranges and needn't reach their ends.
Inputs may be any that keep to these rules, and one draw needn't show every extreme that they name: Distinct values; block k is kept by index unit_slot[k] // 42 of dp; each index holds at most 42 blocks and one holds exactly 42.
All inputs are finite; a program needn't handle non-finite values.
Results may differ from the reference program's by a relative error of at most 0.0062.
The reference program's roundings to bfloat16 on the way count: a program that leaves them out, or rounds other values in their place, can miss the bound.
Values may be sent and summed in bfloat16 or wider, within the bound.
No kernel may reach another device: no remote copies, remote signals or barrier semaphores. Data moves between devices by JAX's collectives and lax.ppermute only.
A program may use at most 576 MiB of HBM per device.

```python
import math
import jax
import jax.numpy as jnp
import numpy as np
from jax import lax

D = 1120
HEADS = 20
HD = 56
FF = 4480
V = 42112
UROWS = 56
PACK = 512
MICRO = 2
SEGS = 4
STEP = 10
MOST = 256
NU = 248
SLOTS = 42
N_DP = 8
N_MP = 4


def slot_table(key):
    total = N_DP * SLOTS
    order = jax.random.permutation(jax.random.fold_in(key, 11), total)
    full_owner = jax.random.randint(jax.random.fold_in(key, 12), (), 0, N_DP)
    owner_of = order // SLOTS
    places = jnp.arange(total, dtype=jnp.int32)
    score = jnp.where(owner_of == full_owner, places - total, places)
    chosen = order[jnp.argsort(score, stable=True)][:NU]
    shuffle = jax.random.permutation(jax.random.fold_in(key, 13), NU)
    return chosen[shuffle].astype(jnp.int32)


def draw_unit_slot(key, part):
    return slot_table(key)


def draw_master(key, part):
    slots = slot_table(key)
    key = jax.random.fold_in(key, 21)
    total = N_DP * SLOTS
    unit_at = jnp.full((total,), -1, jnp.int32).at[slots].set(jnp.arange(NU, dtype=jnp.int32))
    shape = (total, N_MP, UROWS, D)
    raw = jnp.clip(jax.random.normal(key, shape, jnp.float32), -6.0, 6.0)
    top = 3.0
    local_row = jnp.maximum(unit_at, 0)[:, None, None] * UROWS + jnp.arange(UROWS)[None, None, :]
    mp_index = jnp.arange(N_MP)[None, :, None]
    q_rows = HEADS // N_MP * HD
    ff_rows = FF // N_MP
    v_rows = V // N_MP
    base = 1.0 / D ** 0.5
    vocab = (mp_index * v_rows + local_row - 4 * q_rows - 2 * ff_rows).astype(jnp.float32)
    table_scale = (1.0 + (top - 1.0) * vocab / V) * base
    scale = jnp.where(local_row < 3 * q_rows, base, jnp.where(local_row < 4 * q_rows, 6.0 * base, jnp.where(local_row < 4 * q_rows + ff_rows, base, jnp.where(local_row < 4 * q_rows + 2 * ff_rows, 1.0 / FF ** 0.5, table_scale))))
    return (raw * scale[..., None]).reshape(total, N_MP * UROWS, D).astype(jnp.float32)


def draw_counted(key, part):
    key = jax.random.fold_in(key, 31)
    rows = N_DP * MICRO
    level = 250 + 500 * jnp.arange(rows, dtype=jnp.int32) // rows
    roll = jax.random.randint(key, (rows, PACK), 0, 1000)
    return (roll < level[:, None]).astype(jnp.int32)


def draw_norm_params(key, part):
    key = jax.random.fold_in(key, 41)
    raw = jnp.clip(jax.random.normal(key, (6, D), jnp.float32), -6.0, 6.0)
    kind = (jnp.arange(6) % 2)[:, None]
    return jnp.where(kind == 0, 1.0 + 0.15 * raw, 0.3 * raw).astype(jnp.float32)


def touch_ends(array, own_key, low, high):
    shape = array.shape
    spot = [jax.random.randint(jax.random.fold_in(own_key, axis), (), 0, shape[axis]) for axis in range(len(shape))]
    array = array.at[tuple(spot)].set(low)
    longest = shape.index(max(shape))
    spot[longest] = (spot[longest] + 1) % shape[longest]
    return array.at[tuple(spot)].set(high)


def shard_levels(rng, extent, cuts, least, top_value):
    def one(dim, blocks):
        steps = jax.random.uniform(jax.random.fold_in(jax.random.fold_in(rng, 6), dim), (blocks,), jnp.float32, least / len(cuts), top_value / len(cuts))
        return jnp.repeat(jnp.exp(steps), extent[dim] // blocks).reshape((-1,) + (1,) * (len(extent) - dim - 1))

    level = one(*cuts[0])
    for cut in cuts[1:]:
        level = level * one(*cut)
    return level


def rank_table(count, skew):
    loads = [(1 << 20) // math.isqrt(standing ** skew) + 1 for standing in range(1, count + 1)]
    width = 1 + sum(loads) // (1 << 30)
    return np.cumsum(np.array([max(1, weight // width) for weight in loads]))


def ranked(key, extent, count, skew):
    listing = rank_table(count, skew)
    pick = jax.random.randint(jax.random.fold_in(key, 1), extent, 0, int(listing[count - 1]))
    standing = jnp.searchsorted(jnp.asarray(listing, jnp.int32), pick, side="right")
    return jax.random.permutation(jax.random.fold_in(key, 2), count)[standing].astype(jnp.int32)


def split_up(count, total, reach, lean):
    loads = [(1 << 20) // math.isqrt(grade ** lean) + 1 for grade in range(2, count + 1)]
    spare, counts = total - reach - (count - 1), [1] * (count - 1)
    while spare > 0:
        movable = [i for i in range(count - 1) if counts[i] < reach]
        whole, budget = sum([loads[i] for i in movable]), spare
        for i in movable:
            extra = min(reach - counts[i], max(1, budget * loads[i] // whole), spare)
            counts[i] = counts[i] + extra
            spare = spare - extra
    return np.array([reach] + counts)


def uneven_parts(own_key, amount, total, reach, lean):
    if amount == 2:
        one = jax.random.randint(own_key, (), max(1, total - reach), min(reach, total - 1) + 1)
        return jnp.stack([one, total - one])
    sizes = jnp.asarray(split_up(amount, total, reach, lean), jnp.int32)
    twos = (amount - 1) // 2
    source_of, sink = sizes[1:1 + 2 * twos:2], sizes[2:2 + 2 * twos:2]
    slack = jnp.minimum(source_of - 1, reach - sink)
    passed = jax.random.randint(jax.random.fold_in(own_key, 1), (twos,), 0, 1 << 20) % (slack + 1)
    sizes = sizes.at[1:1 + 2 * twos:2].set(source_of - passed).at[2:2 + 2 * twos:2].set(sink + passed)
    return sizes[jax.random.permutation(jax.random.fold_in(own_key, 2), amount)]


def noise(stream_key, shape, width, bound, split=(), held_as=jnp.bfloat16):
    level = shard_levels(stream_key, shape, split, -0.22, 0.18) if split else 1.0
    array = jax.random.normal(stream_key, shape, jnp.float32) * width * level
    return jnp.minimum(jnp.maximum(array, -bound), bound).astype(held_as)


def setup_inputs(seed: int = 0) -> dict:
    seeds = jax.random.split(jax.random.key(seed), 11)
    return {
        "token_ids": touch_ends(ranked(seeds[0], (N_DP * MICRO, PACK), V, 2), jax.random.fold_in(seeds[0], 3), 0, V - 1).astype(jnp.int32),
        "seg_lengths": jax.vmap(lambda own: uneven_parts(own, SEGS, PACK, MOST, 2))(jax.random.split(seeds[1], (N_DP * MICRO))).reshape((N_DP * MICRO, SEGS)).astype(jnp.int32),
        "counted": draw_counted(jax.random.fold_in(seeds[10], 71), 0),
        "unit_slot": draw_unit_slot(jax.random.fold_in(seeds[10], 71), 0),
        "master": draw_master(jax.random.fold_in(seeds[10], 71), 0),
        "first_moment": noise(seeds[5], (N_DP * SLOTS, N_MP * UROWS, D), (0.111 / (NU * N_MP * UROWS * D) ** 0.5), 8.44336100271903e-05, ((0, 8), (1, 4)), jnp.float32),
        "second_moment": jnp.clip(jnp.exp(math.log(3.3752161066047393e-09) - 1.3843914 * jax.random.uniform(seeds[6], (N_DP * SLOTS, N_MP * UROWS, D), jnp.float32) ** shard_levels(seeds[6], (N_DP * SLOTS, N_MP * UROWS, D), ((0, 8), (1, 4)), -0.2, 0.2)), 8.454112410127834e-10, 3.3752161066047393e-09),
        "norm_params": draw_norm_params(jax.random.fold_in(seeds[10], 71), 0),
        "norm_first": noise(seeds[8], (6, D), (0.9 / (NU * N_MP * UROWS * D) ** 0.5), 0.00068459683, (), jnp.float32),
        "norm_second": jnp.clip(jnp.exp(jax.random.uniform(seeds[9], (6, D), jnp.float32, math.log(5.464635322027789e-08), math.log(2.1537093175538757e-07))), 5.464635322027789e-08, 2.1537093175538757e-07),
    }


@jax.custom_vjp
def low(v):
    return lax.optimization_barrier(v.astype(jnp.bfloat16)).astype(jnp.float32)

@jax.custom_vjp
def low_back(v):
    return v

def low_keep(v):
    return (low(v), None)

def low_pass(kept, grad):
    return (grad,)

def back_keep(v):
    return (v, None)

def back_low(kept, grad):
    return (low(grad),)
low.defvjp(low_keep, low_pass)
low_back.defvjp(back_keep, back_low)
NORM_EPS = 1e-05
LEARN_RATE = 0.1
BETA_ONE = 0.9
BETA_TWO = 0.95
ADAM_EPS = 1e-08
WEIGHT_DECAY = 0.1
CLIP_LIMIT = 1.0
NEG_FILL = -1e+30
HIGH = lax.Precision.HIGHEST

def layer_norm(x, gain, shift):
    centred = x - lax.optimization_barrier(jnp.mean(x, axis=-1, keepdims=True))
    scale = lax.rsqrt(lax.optimization_barrier(jnp.mean(centred * centred, axis=-1, keepdims=True)) + NORM_EPS)
    return centred * scale * gain + shift

def segment_ids(lengths, span):
    bounds = jnp.cumsum(lengths)
    return lax.optimization_barrier(jnp.sum(jnp.arange(span)[:, None] >= bounds[None, :], axis=1)).astype(jnp.int32)

def matmul_t(left, right):
    return jnp.dot(left, right.T, precision=HIGH)

def assemble(units):
    local = units.reshape(NU, N_MP, UROWS, D).transpose(1, 0, 2, 3).reshape(N_MP, NU * UROWS, D)
    q_rows = HEADS // N_MP * HD
    ff_rows = FF // N_MP
    edges = [0, q_rows, 2 * q_rows, 3 * q_rows, 4 * q_rows, 4 * q_rows + ff_rows, 4 * q_rows + 2 * ff_rows, NU * UROWS]
    return [local[:, edges[i]:edges[i + 1]].reshape(-1, D) for i in range(7)]

def pack_loss(weights, gains, ids, lengths, marks):
    w_query, w_key, w_value, w_out, w_up, w_down, table = weights
    seg = segment_ids(lengths, PACK)
    x0 = table[ids] * D ** 0.5
    a1 = low(layer_norm(x0, gains[0], gains[1]))
    query = low(low_back(matmul_t(a1, w_query))).reshape(PACK, HEADS, HD)
    keys = low(low_back(matmul_t(a1, w_key))).reshape(PACK, HEADS, HD)
    values = low(low_back(matmul_t(a1, w_value))).reshape(PACK, HEADS, HD)
    raw = jnp.einsum('qhd,khd->hqk', query, keys, precision=HIGH)
    scores = low_back(raw * HD ** (-0.5))
    place = jnp.arange(PACK)
    allowed = (seg[:, None] == seg[None, :]) & (place[None, :] <= place[:, None])
    scores = jnp.where(allowed[None], scores, NEG_FILL)
    probs = jax.nn.softmax(scores, axis=-1)
    mixed = jnp.einsum('hqk,khd->qhd', low(probs), values, precision=HIGH).reshape(PACK, HEADS * HD)
    mixed = low(low_back(mixed))
    x1 = x0 + low_back(jnp.dot(mixed, w_out, precision=HIGH))
    a2 = low(layer_norm(x1, gains[2], gains[3]))
    hidden = low(jax.nn.gelu(low_back(matmul_t(a2, w_up))))
    x2 = x1 + low_back(jnp.dot(hidden, w_down, precision=HIGH))
    final = low(layer_norm(x2, gains[4], gains[5]))
    logits = low_back(matmul_t(final, table))
    lse = jax.nn.logsumexp(logits, axis=-1)
    following = jnp.concatenate([ids[1:], ids[:1]])
    keep = jnp.concatenate([(seg[1:] == seg[:-1]) & (marks[:-1] == 1), jnp.zeros((1,), bool)]).astype(jnp.float32)
    picked = jnp.take_along_axis(logits, following[:, None].astype(jnp.int32), axis=1)[:, 0]
    return (jnp.sum(keep * (lse - picked)), jnp.sum(keep))

def adam_update(weight, grad, first, second, decay):
    first = BETA_ONE * first + (1.0 - BETA_ONE) * grad
    second = BETA_TWO * second + (1.0 - BETA_TWO) * grad * grad
    stride = first / (1.0 - BETA_ONE ** STEP) / (jnp.sqrt(second / (1.0 - BETA_TWO ** STEP)) + ADAM_EPS)
    return (weight - LEARN_RATE * (stride + decay * weight), first, second)

def reference(token_ids, seg_lengths, counted, unit_slot, master, first_moment, second_moment, norm_params, norm_first, norm_second):
    checked = jax.checkpoint(pack_loss)

    def total_loss(units, gains):
        weights = assemble(low(units))

        def one_pack(carry, items):
            loss, count = checked(weights, gains, items[0], items[1], items[2])
            return ((carry[0] + loss, carry[1] + count), None)
        zero = jnp.zeros((), jnp.float32)
        (loss, count), _ = lax.scan(one_pack, (zero, zero), (token_ids, seg_lengths, counted))
        return (loss, count)
    units = master[unit_slot]
    loss_sum, pull, loss_count = jax.vjp(total_loss, units, norm_params, has_aux=True)
    grad_units, grad_gains = pull(jnp.ones((), jnp.float32))
    grad_slots = jnp.zeros_like(master).at[unit_slot].set(grad_units)
    clip_norm = jnp.sqrt(jnp.sum(grad_slots * grad_slots) + jnp.sum(grad_gains * grad_gains))
    factor = jnp.minimum(1.0, CLIP_LIMIT / (clip_norm + 1e-06))
    new_master, new_first, new_second = adam_update(master, factor * grad_slots, first_moment, second_moment, WEIGHT_DECAY)
    new_norms, new_norm_first, new_norm_second = adam_update(norm_params, factor * grad_gains, norm_first, norm_second, 0.0)
    return (new_master, new_first, new_second, new_norms, new_norm_first, new_norm_second, clip_norm, loss_sum, loss_count)
```

```python
import jax
import jax.numpy as jnp
from jax import lax
from jax.sharding import PartitionSpec as P

HEADS = 20
HD = 56
FF = 4480
V = 42112
STEP = 10


NORM_EPS = 1e-05
LEARN_RATE = 0.1
BETA_ONE = 0.9
BETA_TWO = 0.95
ADAM_EPS = 1e-08
WEIGHT_DECAY = 0.1
CLIP_LIMIT = 1.0
NEG_FILL = -1e30

PICK = 64
F32 = jnp.float32
BF16 = jnp.bfloat16


def dp_pair(value):
    size = lax.axis_size("dp")
    return lax.ppermute(value, "dp", [(d, d ^ 1) for d in range(size)])


def dp_right(value):
    size = lax.axis_size("dp")
    return lax.ppermute(value, "dp", [(d, d + 2) for d in range(size - 2)])


def dp_left(value):
    size = lax.axis_size("dp")
    return lax.ppermute(value, "dp", [(d + 2, d) for d in range(size - 2)])


def dp_flip(value, bit):
    size = lax.axis_size("dp")
    return lax.ppermute(value, "dp", [(d, d ^ bit) for d in range(size)])


def mp_flip(value, bit):
    size = lax.axis_size("mp")
    return lax.ppermute(value, "mp", [(d, d ^ bit) for d in range(size)])


def bits_of(axis):
    return [1 << k for k in range(lax.axis_size(axis).bit_length() - 1)]


def rounded(value):
    return lax.reduce_precision(value, 8, 7)


def half_of(value, which):
    count = value.shape[0] // 2
    return lax.dynamic_slice_in_dim(value, which * count, count, 0)


def in_order(mine, other, which):
    first = jnp.where(which == 0, mine, other)
    second = jnp.where(which == 0, other, mine)
    return jnp.concatenate([first, second], axis=0)


def mp_sum(value):
    bits = bits_of("mp")
    core = lax.axis_index("mp") % 2
    total = half_of(value, core) + mp_flip(half_of(value, 1 - core), 1)
    for bit in bits[1:]:
        total = rounded(total)
        total = total + mp_flip(total.astype(BF16), bit).astype(F32)
    return in_order(total, mp_flip(total, 1), core)


def small_sum(value, axes):
    for axis in axes:
        flip = mp_flip if axis == "mp" else dp_flip
        for bit in bits_of(axis):
            value = value + flip(value, bit)
    return value


def ceil_div(a, b):
    return -((-a) // b)


class Layout:
    def __init__(self, slot, slots, per_line):
        owner = slot // slots
        line = lax.axis_size("dp") // 2
        row, col = owner // 2, owner % 2
        key = (col * line + row) * slots + slot % slots
        me = lax.axis_index("dp")
        count = slot.shape[0]
        lines = jnp.arange(2)
        rows = jnp.arange(line)
        before_row = (row[:, None] < rows[None, :])[:, :, None]
        upto_row = (row[:, None] <= rows[None, :])[:, :, None]
        on_line = (col[:, None] == lines[None, :])[:, None, :]
        starts = jnp.sum(before_row & on_line, axis=0).astype(jnp.int32)
        ends = jnp.sum(upto_row & on_line, axis=0).astype(jnp.int32)
        total = ends[-1]
        position = jnp.sum(key[None, :] < key[:, None], axis=1).astype(jnp.int32)
        if per_line:
            base = jnp.zeros((2,), jnp.int32)
            position = position - jnp.where(col == 1, total[0], 0)
        else:
            base = jnp.stack([jnp.zeros((), jnp.int32), total[0]])
        z, x = me // 2, me % 2
        self.low, self.high = base[x], base[x] + total[x]
        self.other_low, self.other_high = base[1 - x], base[1 - x] + total[1 - x]
        self.first, self.last = base[x] + starts[z, x], base[x] + ends[z, x]
        self.longest = jnp.max(total)
        self.position, self.col, self.owner, self.slot = position, col, owner, slot
        self.starts, self.ends, self.total = starts, ends, total
        self.count, self.slots = count, slots
        self.mine = owner == me

    def steps(self, chunk):
        line = self.starts.shape[0]
        rows = jnp.arange(line)[:, None]
        right = ceil_div(self.ends, chunk) + (line - 2 - rows)
        left = ceil_div(self.total[None, :] - self.starts, chunk) + (rows - 1)
        return jnp.maximum(jnp.max(right[:-1]), jnp.max(left[1:])).astype(jnp.int32)

    def unit_at(self, places, mask):
        hit = (self.position[None, :] == jnp.arange(places)[:, None]) & mask[None, :]
        return hit


def window(store, low, chunk):
    start = jnp.clip(low, 0, store.shape[0] - chunk)
    return start, lax.dynamic_slice_in_dim(store, start, chunk, 0)


def put(store, block, low, valid_low, valid_high, add):
    chunk = block.shape[0]
    start, old = window(store, low, chunk)
    place = start + jnp.arange(chunk)
    good = (place >= jnp.maximum(low, valid_low)) & (place < jnp.minimum(low + chunk, valid_high))
    good = good[:, None, None]
    if add:
        new = old + jnp.where(good, block.astype(old.dtype), 0)
    else:
        new = jnp.where(good, block, old)
    return lax.dynamic_update_slice_in_dim(store, new, start, 0)


def edges(lay, k, chunk):
    line = lax.axis_size("dp") // 2
    z = lax.axis_index("dp") // 2
    up_near = lay.low + (k - (line - 2 - z)) * chunk
    up_far = lay.low + (k - (line - 1 - z)) * chunk
    down_near = lay.high - (k - z + 2) * chunk
    down_far = lay.high - (k - z + 1) * chunk
    return up_near, up_far, down_near, down_far


def spread_step(store, lay, k, chunk):
    up_near, up_far, down_near, down_far = edges(lay, k, chunk)
    to_right = dp_right(window(store, up_near, chunk)[1])
    to_left = dp_left(window(store, down_near, chunk)[1])
    store = put(store, to_right, up_far, lay.low, lay.first, False)
    return put(store, to_left, down_far, lay.last, lay.high, False)


def collect_step(store, lay, k, chunk):
    up_near, up_far, down_near, down_far = edges(lay, k, chunk)
    to_left = dp_left(window(store, up_far, chunk)[1].astype(BF16))
    to_right = dp_right(window(store, down_far, chunk)[1].astype(BF16))
    store = put(store, to_left, up_near, lay.low, lay.last, True)
    return put(store, to_right, down_near, lay.first, lay.high, True)


def spread(store, lay, chunk, planned):
    steps = lay.steps(chunk)
    store = lax.fori_loop(
        0,
        jnp.maximum(steps - planned, 0),
        lambda i, s: spread_step(s, lay, steps - 1 - i, chunk),
        store,
    )
    for k in reversed(range(planned)):
        store = spread_step(store, lay, k, chunk)
    return store


def collect(store, lay, chunk, planned):
    steps = lay.steps(chunk)
    for k in range(planned):
        store = collect_step(store, lay, k, chunk)
    return lax.fori_loop(
        planned, jnp.maximum(steps, planned), lambda k, s: collect_step(s, lay, k, chunk), store
    )


def swap_step(store, lay, k, chunk):
    block = dp_pair(window(store, lay.low + k * chunk, chunk)[1])
    return put(store, block, lay.other_low + k * chunk, lay.other_low, lay.other_high, False)


def fold_step(store, lay, k, chunk):
    block = dp_pair(window(store, lay.other_low + k * chunk, chunk)[1].astype(BF16))
    return put(store, block, lay.low + k * chunk, lay.low, lay.high, True)


def pair_steps(step, store, lay, chunk, planned):
    steps = ceil_div(lay.longest, chunk)
    for k in range(planned):
        store = step(store, lay, k, chunk)
    return lax.fori_loop(
        planned, jnp.maximum(steps, planned), lambda k, s: step(s, lay, k, chunk), store
    )


def layer_norm(x, gain, shift):
    centred = x - jnp.mean(x, axis=-1, keepdims=True)
    scale = lax.rsqrt(jnp.mean(centred * centred, axis=-1, keepdims=True) + NORM_EPS)
    return centred * scale * gain + shift


def segment_ids(lengths, span):
    bounds = jnp.cumsum(lengths, axis=-1)
    return jnp.sum(jnp.arange(span)[None, :, None] >= bounds[:, None, :], axis=-1)


def dot_t(left, right):
    return lax.dot_general(left, right, (((1,), (1,)), ((), ())), preferred_element_type=F32)


def dot_first(left, right):
    return lax.dot_general(left, right, (((0,), (0,)), ((), ())), preferred_element_type=F32)


def dot_plain(left, right):
    return jnp.dot(left, right, preferred_element_type=F32)


def attention_probs(query, keys, seg):
    span = seg.shape[1]
    scores = jnp.einsum("bqhd,bkhd->bhqk", query, keys, preferred_element_type=F32) * HD ** (-0.5)
    place = jnp.arange(span)
    allowed = (seg[:, :, None] == seg[:, None, :]) & (place[None, None, :] <= place[None, :, None])
    scores = jnp.where(allowed[:, None], scores, NEG_FILL)
    expo = jnp.exp(scores - jnp.max(scores, axis=-1, keepdims=True))
    return expo / jnp.sum(expo, axis=-1, keepdims=True)


def attention_part(x0, seg, gains, w_qkv, w_out, heads):
    packs, span = seg.shape
    a1b = layer_norm(x0, gains[0], gains[1]).astype(BF16)
    qkv = dot_t(a1b, w_qkv).astype(BF16).reshape(packs, span, 3, heads, HD)
    probs = attention_probs(qkv[:, :, 0], qkv[:, :, 1], seg)
    mixed = jnp.einsum(
        "bhqk,bkhd->bqhd", probs.astype(BF16), qkv[:, :, 2], preferred_element_type=F32
    )
    mixed = mixed.reshape(packs * span, heads * HD).astype(BF16)
    x1 = x0 + mp_sum(dot_plain(mixed, w_out))
    return x1, (a1b, qkv, probs, mixed)


def mlp_part(x1, gains, w_up, w_down):
    a2b = layer_norm(x1, gains[2], gains[3]).astype(BF16)
    pre = dot_t(a2b, w_up)
    hidden = jax.nn.gelu(pre).astype(BF16)
    x2 = x1 + mp_sum(dot_plain(hidden, w_down))
    return x2, (a2b, pre, hidden)


def mlp_back(dx2, x1, gains, w_up, w_down, saved):
    a2b, pre, hidden = saved
    dz = dx2.astype(BF16)
    d_hidden = dot_t(dz, w_down)
    d_pre = jax.vjp(jax.nn.gelu, pre)[1](d_hidden)[0].astype(BF16)
    d_a2 = mp_sum(dot_plain(d_pre, w_up))
    d_down = dot_first(hidden, dz)
    d_up = dot_first(d_pre, a2b)
    dx1_norm, d_g2, d_b2 = jax.vjp(layer_norm, x1, gains[2], gains[3])[1](d_a2)
    return dx2 + dx1_norm, (d_up, d_down), (d_g2, d_b2)


def attention_back(dx1, x0, gains, w_qkv, w_out, heads, saved, packs):
    a1b, qkv, kept, mixed = saved
    span = x0.shape[0] // packs
    query, keys, values = qkv[:, :, 0], qkv[:, :, 1], qkv[:, :, 2]
    dy = dx1.astype(BF16)
    d_mixed = dot_t(dy, w_out).astype(BF16).reshape(packs, span, heads, HD)
    d_probs = jnp.einsum("bqhd,bkhd->bhqk", d_mixed, values, preferred_element_type=F32)
    d_values = jnp.einsum(
        "bhqk,bqhd->bkhd", kept.astype(BF16), d_mixed, preferred_element_type=F32
    )
    d_scores = (kept * (d_probs - jnp.sum(kept * d_probs, axis=-1, keepdims=True))).astype(BF16)
    d_query = jnp.einsum("bhqk,bkhd->bqhd", d_scores, keys, preferred_element_type=F32) * HD ** (
        -0.5
    )
    d_keys = jnp.einsum("bhqk,bqhd->bkhd", d_scores, query, preferred_element_type=F32) * HD ** (
        -0.5
    )
    d_qkv = (
        jnp.stack([d_query, d_keys, d_values], axis=2)
        .reshape(packs * span, 3 * heads * HD)
        .astype(BF16)
    )
    d_a1 = mp_sum(dot_plain(d_qkv, w_qkv))
    d_out = dot_first(mixed, dy)
    d_qkv_weight = dot_first(d_qkv, a1b)
    dx0_norm, d_g1, d_b1 = jax.vjp(layer_norm, x0, gains[0], gains[1])[1](d_a1)
    return dx1 + dx0_norm, (d_qkv_weight, d_out), (d_g1, d_b1)


def adam_update(weight, grad, first, second, decay):
    first = BETA_ONE * first + (1.0 - BETA_ONE) * grad
    second = BETA_TWO * second + (1.0 - BETA_TWO) * grad * grad
    stride = first / (1.0 - BETA_ONE**STEP) / (jnp.sqrt(second / (1.0 - BETA_TWO**STEP)) + ADAM_EPS)
    return (weight - LEARN_RATE * (stride + decay * weight), first, second)


def merge_stats(left, right):
    top = jnp.maximum(left[0], right[0])
    total = left[1] * jnp.exp(left[0] - top) + right[1] * jnp.exp(right[0] - top)
    return jnp.stack([top, total, left[2] + right[2]])


def per_device(
    token_ids,
    seg_lengths,
    counted,
    unit_slot,
    master,
    first_moment,
    second_moment,
    norm_params,
    norm_first,
    norm_second,
):
    slots, rows_unit, width = master.shape
    dp = lax.axis_size("dp")
    parts = lax.axis_size("mp")
    me = lax.axis_index("dp")
    piece = lax.axis_index("mp")
    heads = HEADS // parts
    q_rows = heads * HD
    ff_rows = FF // parts
    vocab_rows = V // parts
    a_units = 4 * q_rows // rows_unit
    f_units = 2 * ff_rows // rows_unit
    e_units = vocab_rows // rows_unit
    packs, span = token_ids.shape
    tokens = packs * span
    root = width**0.5
    line = dp // 2

    lay_a = Layout(unit_slot[:a_units], slots, False)
    lay_f = Layout(unit_slot[a_units : a_units + f_units], slots, False)
    lay_e = Layout(unit_slot[a_units + f_units :], slots, True)
    most = min(e_units, line * slots)
    usual = min(most, 8 * (ceil_div(e_units * 19, 2 * 16) // 8))

    packed = jnp.concatenate([token_ids, seg_lengths, counted], axis=1)
    packed = lax.all_gather(packed, "dp", axis=0, tiled=False)

    def run(e_room):
        own = master.astype(BF16)

        def start_store(lay, places):
            hit = lay.unit_at(places, lay.mine)
            index = jnp.sum(jnp.where(hit, (lay.slot % slots)[None, :], 0), axis=1)
            return own[index]

        ids_all = packed[:, :, :span].reshape(dp, tokens)
        piece_all = ids_all // vocab_rows
        local_all = ids_all % vocab_rows
        block_all = local_all // rows_unit
        slot_all = jnp.sum(
            jnp.where(
                block_all[:, :, None] == jnp.arange(e_units)[None, None, :],
                lay_e.slot[None, None, :],
                0,
            ),
            axis=-1,
        )
        code_all = piece_all * dp + slot_all // slots
        order = jnp.arange(tokens)
        earlier = order[None, None, :] < order[None, :, None]
        repeat = jnp.any((ids_all[:, :, None] == ids_all[:, None, :]) & earlier, axis=-1)
        first_all = ~repeat
        rank_all = jnp.sum(
            (code_all[:, :, None] == code_all[:, None, :]) & earlier & first_all[:, None, :],
            axis=-1,
        ).astype(jnp.int32)
        rounds = jnp.max(jnp.where(first_all, rank_all, 0)) // PICK + 1
        mine_all = first_all & (code_all == piece * dp + me)
        row_all = (slot_all % slots) * rows_unit + local_all % rows_unit
        ids_own = token_ids.reshape(tokens)
        own_view = lambda array: lax.dynamic_index_in_dim(array, me, 0, False)
        code_own = own_view(code_all)
        rank_own = jnp.sum(
            jnp.where(
                (ids_own[:, None] == ids_own[None, :]) & own_view(first_all)[None, :],
                own_view(rank_all)[None, :],
                0,
            ),
            axis=-1,
        )
        inside_own = (code_own // dp) == piece
        owner_own = code_own % dp

        def owner_picks(turn):
            wanted = turn * PICK + jnp.arange(PICK)
            hit = mine_all[:, None, :] & (rank_all[:, None, :] == wanted[None, :, None])
            row = jnp.sum(jnp.where(hit, row_all[:, None, :] + 1, 0), axis=-1) - 1
            return (
                row.reshape(dp * PICK)[:, None] == jnp.arange(slots * rows_unit)[None, :]
            ).astype(BF16)

        def token_picks(turn):
            rank = rank_own - turn * PICK
            good = inside_own & (rank >= 0) & (rank < PICK)
            key = jnp.where(good, owner_own * PICK + rank, -1)
            return (key[:, None] == jnp.arange(dp * PICK)[None, :]).astype(BF16)

        def lookup(turn):
            rows = dot_plain(owner_picks(turn), own.reshape(slots * rows_unit, width)).astype(BF16)
            rows = lax.all_to_all(rows.reshape(dp, PICK, width), "dp", 0, 0)
            return dot_plain(token_picks(turn), rows.reshape(dp * PICK, width))

        x0 = lax.fori_loop(1, rounds, lambda i, t: t + lookup(i), lookup(0))
        x0 = mp_sum(x0) * root

        store_a = spread(start_store(lay_a, a_units), lay_a, 4, 4)
        store_a = pair_steps(swap_step, store_a, lay_a, 4, 3)
        store_f = spread(start_store(lay_f, f_units), lay_f, 6, 4)
        store_f = pair_steps(swap_step, store_f, lay_f, 6, 4)
        store_e = spread(start_store(lay_e, e_room), lay_e, 8, 10)
        w_a = store_a[lay_a.position].reshape(a_units * rows_unit, width)
        w_f = store_f[lay_f.position].reshape(f_units * rows_unit, width)
        w_qkv, w_out = w_a[: 3 * q_rows], w_a[3 * q_rows :]
        w_up, w_down = w_f[:ff_rows], w_f[ff_rows:]
        table = store_e.reshape(e_room * rows_unit, width)

        seg = segment_ids(seg_lengths, span)
        x1, saved_a = attention_part(x0, seg, norm_params, w_qkv, w_out, heads)
        x2, saved_f = mlp_part(x1, norm_params, w_up, w_down)
        final_low = layer_norm(x2, norm_params[4], norm_params[5]).astype(BF16)

        core = piece % 2
        theirs = dp_pair(half_of(final_low, core))
        theirs = in_order(theirs, mp_flip(theirs, 1), core)
        both = jnp.concatenate([final_low, theirs], axis=0)
        pair_data = jnp.stack([own_view(packed), lax.dynamic_index_in_dim(packed, me ^ 1, 0, False)])
        pair_ids = pair_data[:, :, :span]
        pair_seg = segment_ids(
            pair_data[:, :, span : span + seg_lengths.shape[1]].reshape(2 * packs, -1), span
        ).reshape(2, packs, span)
        pair_counted = pair_data[:, :, span + seg_lengths.shape[1] :]
        keep = jnp.concatenate(
            [
                (pair_seg[:, :, 1:] == pair_seg[:, :, :-1]) & (pair_counted[:, :, :-1] == 1),
                jnp.zeros((2, packs, 1), bool),
            ],
            axis=2,
        ).astype(F32)
        keep = keep.reshape(2 * tokens)
        target = jnp.concatenate([pair_ids[:, :, 1:], pair_ids[:, :, :1]], axis=2)
        target = target.reshape(2 * tokens)
        t_local = target % vocab_rows
        here = (lay_e.col == me % 2)[None, :] & (
            (t_local // rows_unit)[:, None] == jnp.arange(e_units)[None, :]
        )
        t_block = jnp.sum(jnp.where(here, lay_e.position[None, :] + 1, 0), axis=1) - 1
        t_row = jnp.where(
            (target // vocab_rows == piece) & (t_block >= 0),
            t_block * rows_unit + t_local % rows_unit,
            -1,
        )
        limit = lay_e.high * rows_unit
        place = jnp.arange(e_room * rows_unit)
        real = (place < limit)[None, :]
        onehot = place[None, :] == t_row[:, None]

        logits = dot_t(both, table)
        top = jnp.max(jnp.where(real, logits, NEG_FILL), axis=-1)
        total = jnp.sum(jnp.where(real, jnp.exp(logits - top[:, None]), 0.0), axis=-1)
        picked = jnp.sum(jnp.where(onehot, logits, 0.0), axis=-1)
        stats = jnp.stack([top, total, picked])
        for bit in bits_of("mp"):
            stats = merge_stats(stats, mp_flip(stats, bit))
        their_stats = dp_pair(stats)
        their_stats = jnp.concatenate([their_stats[:, tokens:], their_stats[:, :tokens]], axis=1)
        stats = merge_stats(stats, their_stats)
        lse = stats[0] + jnp.log(stats[1])
        loss_sum = jnp.sum((keep * (lse - stats[2]))[:tokens])
        loss_count = jnp.sum(keep[:tokens])
        d_logits = (
            keep[:, None]
            * (jnp.where(real, jnp.exp(logits - lse[:, None]), 0.0) - onehot.astype(F32))
        ).astype(BF16)
        d_final = dot_plain(d_logits, table).reshape(2, tokens, width)
        swapped = mp_flip(
            lax.dynamic_slice_in_dim(d_final, (1 - core) * (tokens // 2), tokens // 2, 1), 1
        )
        part = lax.dynamic_slice_in_dim(d_final, core * (tokens // 2), tokens // 2, 1) + swapped
        part = part[0] + dp_pair(part[1].astype(BF16)).astype(F32)
        for bit in bits_of("mp")[1:]:
            part = rounded(part)
            part = part + mp_flip(part.astype(BF16), bit).astype(F32)
        d_final = in_order(part, mp_flip(part, 1), core)
        grad_e = dot_first(d_logits, both).reshape(e_room, rows_unit, width)
        grad_e = collect(grad_e, lay_e, 8, 10)

        dx2, d_gf, d_bf = jax.vjp(layer_norm, x2, norm_params[4], norm_params[5])[1](d_final)
        dx1, (d_up, d_down), (d_g2, d_b2) = mlp_back(
            dx2, x1, norm_params, w_up, w_down, saved_f
        )

        def sorted_blocks(lay, grad):
            hit = lay.unit_at(lay.count, jnp.ones((lay.count,), bool))
            index = jnp.sum(jnp.where(hit, jnp.arange(lay.count)[None, :], 0), axis=1)
            return grad.reshape(lay.count, rows_unit, width)[index]

        grad_f = sorted_blocks(lay_f, jnp.concatenate([d_up, d_down], axis=0))
        grad_f = pair_steps(fold_step, grad_f, lay_f, 6, 4)
        grad_f = collect(grad_f, lay_f, 6, 4)
        dx0, (d_qkv, d_out), (d_g1, d_b1) = attention_back(
            dx1, x0, norm_params, w_qkv, w_out, heads, saved_a, packs
        )
        grad_a = sorted_blocks(lay_a, jnp.concatenate([d_qkv, d_out], axis=0))
        grad_a = pair_steps(fold_step, grad_a, lay_a, 4, 3)
        grad_a = collect(grad_a, lay_a, 4, 4)

        d_rows = dx0 * root
        d_high = rounded(d_rows)
        d_low = (d_rows - d_high).astype(BF16)
        d_high = d_high.astype(BF16)

        def give_back(turn):
            picks = token_picks(turn)
            rows = (dot_first(picks, d_high) + dot_first(picks, d_low)).astype(BF16)
            rows = lax.all_to_all(rows.reshape(dp, PICK, width), "dp", 0, 0)
            return dot_first(owner_picks(turn), rows.reshape(dp * PICK, width))

        owned = lax.fori_loop(1, rounds, lambda i, t: t + give_back(i), give_back(0))
        owned = owned.reshape(slots, rows_unit, width)
        for lay, grad in ((lay_a, grad_a), (lay_f, grad_f), (lay_e, grad_e)):
            hit = lay.mine[None, :] & ((lay.slot % slots)[None, :] == jnp.arange(slots)[:, None])
            index = jnp.sum(jnp.where(hit, lay.position[None, :], 0), axis=1)
            present = jnp.any(hit, axis=1)[:, None, None]
            owned = owned + jnp.where(present, grad[index], 0.0)

        gain_grads = jnp.stack([d_g1, d_b1, d_g2, d_b2, d_gf, d_bf])
        gain_grads, loss_sum, loss_count = lax.psum((gain_grads, loss_sum, loss_count), "dp")
        owner_squares = small_sum(jnp.sum(owned * owned), ("mp", "dp"))
        clip_norm = jnp.sqrt(owner_squares + jnp.sum(gain_grads * gain_grads))
        factor = jnp.minimum(1.0, CLIP_LIMIT / (clip_norm + 1e-06))
        new_master, new_first, new_second = adam_update(
            master, factor * owned, first_moment, second_moment, WEIGHT_DECAY
        )
        new_norms, new_norm_first, new_norm_second = adam_update(
            norm_params, factor * gain_grads, norm_first, norm_second, 0.0
        )
        return (
            new_master,
            new_first,
            new_second,
            new_norms,
            new_norm_first,
            new_norm_second,
            clip_norm,
            loss_sum,
            loss_count,
        )

    if usual == most:
        return run(most)
    return lax.cond(lay_e.longest <= usual, lambda: run(usual), lambda: run(most))


def solution(mesh):
    placed = (
        P("dp", None),
        P("dp", None),
        P("dp", None),
        P(),
        P("dp", "mp", None),
        P("dp", "mp", None),
        P("dp", "mp", None),
        P(),
        P(),
        P(),
    )
    return jax.shard_map(
        per_device,
        mesh=mesh,
        in_specs=placed,
        out_specs=(
            P("dp", "mp", None),
            P("dp", "mp", None),
            P("dp", "mp", None),
            P(),
            P(),
            P(),
            P(),
            P(),
            P(),
        ),
        check_vma=False,
    )
```

```python
import jax
import jax.numpy as jnp
from jax import lax
from jax.experimental import pallas as pl
from jax.experimental.pallas import tpu as pltpu
from jax.sharding import PartitionSpec as P

HEADS = 20
HD = 56
FF = 4480
V = 42112
STEP = 10


NORM_EPS = 1e-05
LEARN_RATE = 0.1
BETA_ONE = 0.9
BETA_TWO = 0.95
ADAM_EPS = 1e-08
WEIGHT_DECAY = 0.1
CLIP_LIMIT = 1.0
NEG_FILL = -1e30

PICK = 64
F32 = jnp.float32
BF16 = jnp.bfloat16


def dp_pair(value):
    size = lax.axis_size("dp")
    return lax.ppermute(value, "dp", [(d, d ^ 1) for d in range(size)])


def line_hop(value, lane):
    dp, mp = lax.axis_size("dp"), lax.axis_size("mp")
    moves = []
    for d in range(dp):
        for m in range(mp):
            to = d + 2 if (m + lane) % 2 == 0 else d - 2
            if 0 <= to < dp:
                moves.append((d * mp + m, to * mp + m))
    return lax.ppermute(value, ("dp", "mp"), moves)


def dp_flip(value, bit):
    size = lax.axis_size("dp")
    return lax.ppermute(value, "dp", [(d, d ^ bit) for d in range(size)])


def mp_flip(value, bit):
    size = lax.axis_size("mp")
    return lax.ppermute(value, "mp", [(d, d ^ bit) for d in range(size)])


def bits_of(axis):
    return [1 << k for k in range(lax.axis_size(axis).bit_length() - 1)]


def rounded(value):
    return lax.reduce_precision(value, 8, 7)


def half_of(value, which):
    count = value.shape[0] // 2
    return lax.dynamic_slice_in_dim(value, which * count, count, 0)


def in_order(mine, other, which):
    first = jnp.where(which == 0, mine, other)
    second = jnp.where(which == 0, other, mine)
    return jnp.concatenate([first, second], axis=0)


def mp_sum(value, exact=False, stops=()):
    stops = list(stops) + [None] * 3

    def hop(sent, bit, stop):
        got = mp_flip(sent, bit)
        return got if stop is None else stop(got)

    core = lax.axis_index("mp") % 2
    total = half_of(value, core)
    other = half_of(value, 1 - core)
    total = total + hop(other, 1, stops[0])
    for bit in bits_of("mp")[1:]:
        if exact:
            total = total + hop(total, bit, stops[1])
        else:
            total = rounded(total)
            total = total + hop(total.astype(BF16), bit, stops[1]).astype(F32)
    return in_order(total, hop(total, 1, stops[2]), core)


def small_sum(value, axes):
    for axis in axes:
        flip = mp_flip if axis == "mp" else dp_flip
        for bit in bits_of(axis):
            value = value + flip(value, bit)
    return value


def small_gather(value):
    value = value[None]
    me = lax.axis_index("dp")
    for bit in bits_of("dp"):
        value = in_order(value, dp_flip(value, bit), (me // bit) % 2)
    return value


def together(*values):
    return lax.optimization_barrier(values)


def ceil_div(a, b):
    return -((-a) // b)


class Layout:
    def __init__(self, slot, slots, per_line):
        owner = slot // slots
        line = lax.axis_size("dp") // 2
        row, col = owner // 2, owner % 2
        key = (col * line + row) * slots + slot % slots
        me = lax.axis_index("dp")
        rows = jnp.arange(line)
        on_line = (col[:, None] == jnp.arange(2)[None, :])[:, :, None]
        before = on_line & (row[:, None] < rows[None, :])[:, None, :]
        upto = on_line & (row[:, None] <= rows[None, :])[:, None, :]
        self.starts = jnp.sum(before, axis=0).astype(jnp.int32)
        self.ends = jnp.sum(upto, axis=0).astype(jnp.int32)
        self.total = self.ends[:, -1]
        self.base = jnp.zeros((2,), jnp.int32)
        position = jnp.sum(key[None, :] < key[:, None], axis=1).astype(jnp.int32)
        if per_line:
            position = position - jnp.where(col == 1, self.total[0], 0)
        else:
            self.base = self.total[0] * jnp.arange(2)
        self.position, self.col, self.local = position, col, slot % slots
        self.slot, self.count = slot, slot.shape[0]
        self.mine = owner == me
        self.place()

    def place(self):
        me = lax.axis_index("dp")
        z, x = me // 2, me % 2
        self.low, self.other_low = self.base[x], self.base[1 - x]
        self.high, self.other_high = self.low + self.total[x], self.other_low + self.total[1 - x]
        self.first, self.last = self.low + self.starts[x, z], self.low + self.ends[x, z]
        self.longest = jnp.max(self.total)

    def part(self, low, room):
        cut = object.__new__(Layout)
        cut.__dict__.update(self.__dict__)
        cut.starts = jnp.clip(self.starts - low, 0, room)
        cut.ends = jnp.clip(self.ends - low, 0, room)
        cut.total = jnp.clip(self.total - low, 0, room)
        inside = (self.position >= low) & (self.position < low + room)
        cut.position = jnp.where(inside, self.position - low, -1)
        cut.place()
        return cut

    def steps(self, chunk):
        rows = jnp.arange(self.starts.shape[1])
        last = self.starts.shape[1] - 1
        right = ceil_div(self.ends, chunk) + (last - 1 - rows)[None, :]
        left = ceil_div(self.total[:, None] - self.starts, chunk) + (rows - 1)[None, :]
        return jnp.maximum(jnp.max(right[:, :last]), jnp.max(left[:, 1:])).astype(jnp.int32)

    def local_at(self, places):
        hit = (self.position[None, :] == jnp.arange(places)[:, None]) & self.mine[None, :]
        return jnp.sum(jnp.where(hit, self.local[None, :], 0), axis=1)

    def unit_at(self):
        hit = self.position[None, :] == jnp.arange(self.count)[:, None]
        return jnp.sum(jnp.where(hit, jnp.arange(self.count)[None, :], 0), axis=1)

    def at_slot(self, slots):
        hit = self.mine[None, :] & (self.local[None, :] == jnp.arange(slots)[:, None])
        return jnp.sum(jnp.where(hit, self.position[None, :] + 1, 0), axis=1) - 1


def window(store, low, chunk):
    start = jnp.clip(low, 0, store.shape[0] - chunk)
    return start, lax.dynamic_slice_in_dim(store, start, chunk, 0)


def put(store, block, low, valid_low, valid_high, add):
    chunk = block.shape[0]
    start, old = window(store, low, chunk)
    least = jnp.maximum(low, valid_low) - start
    limit = jnp.minimum(low + chunk, valid_high) - start
    place = lax.broadcasted_iota(jnp.int32, block.shape, 0)
    good = (place >= least) & (place < limit)
    if add:
        new = old + jnp.where(good, block.astype(old.dtype), 0)
    else:
        new = jnp.where(good, block, old)
    return lax.dynamic_update_slice_in_dim(store, new, start, 0)


class Stream:
    lanes = 1

    def __init__(self, store, lay, chunk, planned):
        self.store, self.lay, self.chunk, self.planned = store, lay, chunk, planned
        self.needed = jnp.where(lay.longest > 0, self.count_steps(), 0)
        self.done = 0
        self.flight = [None] * self.lanes
        self.prepare()

    def prepare(self):
        pass

    def one(self, store, k):
        blocks = [self.send(self.outgoing(store, k, n), n) for n in range(self.lanes)]
        for n in range(self.lanes):
            store = self.receive(store, blocks[n], k, n)
        return store

    def fly(self, lane, k, value):
        out = self.outgoing(self.store, k, lane)
        self.flight[lane] = self.send(out, lane)
        return value

    def fetch(self, lane, value):
        block = self.flight[lane]
        self.store = self.receive(self.store, block, self.k, lane)
        return value

    def launch(self, value=None):
        self.k = self.order(self.done)
        self.done += 1
        for lane in range(self.lanes):
            value = self.fly(lane, self.k, value)
        return value

    def land(self, value=None):
        for lane in range(self.lanes):
            value = self.fetch(lane, value)
        return value

    def step(self, value=None):
        k = self.order(self.done)
        self.done += 1
        for lane in range(self.lanes):
            value = self.fetch(lane, value)
            value = self.fly(lane, k, value)
        self.k = k
        return value

    def finish(self):
        assert self.done == self.planned
        self.rest()
        return self.store

    def order(self, n):
        return n

    def rest(self):
        self.store = lax.fori_loop(
            self.planned,
            jnp.maximum(self.needed, self.planned),
            lambda k, store: self.one(store, k),
            self.store,
        )


class LineStream(Stream):
    lanes = 2

    def count_steps(self):
        return self.lay.steps(self.chunk)

    def edges(self, k, lane):
        line = lax.axis_size("dp") // 2
        z = lax.axis_index("dp") // 2
        up = (lax.axis_index("mp") + lane) % 2 == 0
        lay, chunk = self.lay, self.chunk
        up_near = lay.low + (k - (line - 2 - z)) * chunk
        down_near = lay.high - (k - z + 2) * chunk
        near = jnp.where(up, up_near, down_near)
        return near, jnp.where(up, up_near - chunk, down_near + chunk), up


class Spread(LineStream):
    def prepare(self):
        self.store = lax.fori_loop(
            0,
            jnp.maximum(self.needed - self.planned, 0),
            lambda i, store: self.one(store, self.needed - 1 - i),
            self.store,
        )

    def order(self, n):
        return self.planned - 1 - n

    def rest(self):
        pass

    def outgoing(self, store, k, lane):
        return window(store, self.edges(k, lane)[0], self.chunk)[1]

    def send(self, out, lane):
        return line_hop(out, lane)

    def receive(self, store, block, k, lane):
        _, far, up = self.edges(k, lane)
        low = jnp.where(up, self.lay.low, self.lay.last)
        high = jnp.where(up, self.lay.first, self.lay.high)
        return put(store, block, far, low, high, False)


class Collect(LineStream):
    def outgoing(self, store, k, lane):
        return window(store, self.edges(k, lane)[1], self.chunk)[1].astype(BF16)

    def send(self, out, lane):
        return line_hop(out, 1 - lane)

    def receive(self, store, block, k, lane):
        near, _, up = self.edges(k, lane)
        low = jnp.where(up, self.lay.low, self.lay.first)
        high = jnp.where(up, self.lay.last, self.lay.high)
        return put(store, block, near, low, high, True)


class PairStream(Stream):
    def count_steps(self):
        return ceil_div(self.lay.longest, self.chunk)

    def send(self, out, lane):
        return dp_pair(out)


class Swap(PairStream):
    def outgoing(self, store, k, lane):
        return window(store, self.lay.low + k * self.chunk, self.chunk)[1]

    def receive(self, store, block, k, lane):
        lay = self.lay
        low = lay.other_low + k * self.chunk
        return put(store, block, low, lay.other_low, lay.other_high, False)


class Fold(PairStream):
    def outgoing(self, store, k, lane):
        low = self.lay.other_low + k * self.chunk
        return window(store, low, self.chunk)[1].astype(BF16)

    def receive(self, store, block, k, lane):
        lay = self.lay
        return put(store, block, lay.low + k * self.chunk, lay.low, lay.high, True)


def layer_norm(x, gain, shift):
    centred = x - jnp.mean(x, axis=-1, keepdims=True)
    scale = lax.rsqrt(jnp.mean(centred * centred, axis=-1, keepdims=True) + NORM_EPS)
    return centred * scale * gain + shift


def segment_ids(lengths, span):
    bounds = jnp.cumsum(lengths, axis=-1)
    return jnp.sum(jnp.arange(span)[None, :, None] >= bounds[:, None, :], axis=-1)


def dot_t(left, right):
    return lax.dot_general(left, right, (((1,), (1,)), ((), ())), preferred_element_type=F32)


def dot_first(left, right):
    return lax.dot_general(left, right, (((0,), (0,)), ((), ())), preferred_element_type=F32)


def dot_plain(left, right):
    return jnp.dot(left, right, preferred_element_type=F32)


def attention_probs(query, keys, seg):
    span = seg.shape[1]
    scores = jnp.einsum("bqhd,bkhd->bhqk", query, keys, preferred_element_type=F32) * HD ** (-0.5)
    place = jnp.arange(span)
    allowed = (seg[:, :, None] == seg[:, None, :]) & (place[None, None, :] <= place[None, :, None])
    scores = jnp.where(allowed[:, None], scores, NEG_FILL)
    expo = jnp.exp(scores - jnp.max(scores, axis=-1, keepdims=True))
    return expo / jnp.sum(expo, axis=-1, keepdims=True)


def assemble_kernel(kind_ref, e_at, f_at, a_at, rows_ref, e_ref, f_ref, a_ref, out_ref, sq_ref):
    slot = pl.program_id(0)
    kind = kind_ref[slot]
    value = jnp.where(kind == 0, e_ref[...], 0.0)
    value = jnp.where(kind == 1, f_ref[...], value)
    value = rows_ref[...] + jnp.where(kind == 2, a_ref[...], value)
    out_ref[...] = value

    @pl.when(slot == 0)
    def _():
        sq_ref[...] = jnp.zeros(sq_ref.shape, F32)

    _, rows, width = value.shape
    sq_ref[...] += jnp.sum((value * value).reshape(rows // 8, 8, width), axis=0)


def assemble(rows, grads, index):
    slots, rows_unit, width = rows.shape
    kind = jnp.full((slots,), 3, jnp.int32)
    for number, at in enumerate(index):
        kind = jnp.where(at >= 0, number, kind)
    index = [jnp.maximum(at, 0).astype(jnp.int32) for at in index]
    block = (1, rows_unit, width)
    return pl.pallas_call(
        assemble_kernel,
        grid_spec=pltpu.PrefetchScalarGridSpec(
            num_scalar_prefetch=4,
            grid=(slots,),
            in_specs=[
                pl.BlockSpec(block, lambda s, k, e, f, a: (s, 0, 0)),
                pl.BlockSpec(block, lambda s, k, e, f, a: (e[s], 0, 0)),
                pl.BlockSpec(block, lambda s, k, e, f, a: (f[s], 0, 0)),
                pl.BlockSpec(block, lambda s, k, e, f, a: (a[s], 0, 0)),
            ],
            out_specs=[
                pl.BlockSpec(block, lambda s, k, e, f, a: (s, 0, 0)),
                pl.BlockSpec((8, width), lambda s, k, e, f, a: (0, 0)),
            ],
        ),
        out_shape=[
            jax.ShapeDtypeStruct(rows.shape, F32),
            jax.ShapeDtypeStruct((8, width), F32),
        ],
    )(kind, *index, rows, *grads)


def when(wanted, work, value, *given):
    def turn(i, so_far):
        i, *held = together(i, *given)
        return work(so_far, *held)

    return lax.fori_loop(0, wanted.astype(jnp.int32), turn, value)


def adam_update(weight, grad, first, second, decay):
    first = BETA_ONE * first + (1.0 - BETA_ONE) * grad
    second = BETA_TWO * second + (1.0 - BETA_TWO) * grad * grad
    stride = first / (1.0 - BETA_ONE**STEP) / (jnp.sqrt(second / (1.0 - BETA_TWO**STEP)) + ADAM_EPS)
    return (weight - LEARN_RATE * (stride + decay * weight), first, second)


def merge_stats(left, right):
    top = jnp.maximum(left[0], right[0])
    total = left[1] * jnp.exp(left[0] - top) + right[1] * jnp.exp(right[0] - top)
    return jnp.stack([top, total, left[2] + right[2]])


def per_device(
    token_ids,
    seg_lengths,
    counted,
    unit_slot,
    master,
    first_moment,
    second_moment,
    norm_params,
    norm_first,
    norm_second,
):
    slots, rows_unit, width = master.shape
    dp = lax.axis_size("dp")
    parts = lax.axis_size("mp")
    me = lax.axis_index("dp")
    piece = lax.axis_index("mp")
    heads = HEADS // parts
    q_rows = heads * HD
    ff_rows = FF // parts
    vocab_rows = V // parts
    a_units = 4 * q_rows // rows_unit
    f_units = 2 * ff_rows // rows_unit
    e_units = vocab_rows // rows_unit
    packs, span = token_ids.shape
    tokens = packs * span
    root = width**0.5
    line = dp // 2

    a_end, f_end = a_units, a_units + f_units
    lay_a = Layout(unit_slot[:a_end], slots, False)
    lay_f = Layout(unit_slot[a_end:f_end], slots, False)
    lay_e = Layout(unit_slot[f_end:], slots, True)
    most = min(e_units, line * slots)
    usual = min(most, 112)
    crowded = lay_e.longest > usual
    lay_m = lay_e.part(0, usual)
    lay_t = lay_e.part(usual, most - usual) if most > usual else None

    own = master.astype(BF16)

    at_a, at_f, at_e = lay_a.local_at(a_units), lay_f.local_at(f_units), lay_m.local_at(usual)
    spread_a = Spread(master[at_a].astype(BF16), lay_a, 5, 3)
    at_f = spread_a.launch(at_f)
    spread_f = Spread(own[at_f], lay_f, 9, 3)
    at_e = spread_f.launch(at_e)
    spread_e = Spread(own[at_e], lay_m, 21, 4)
    spread_e.launch()
    packed = small_gather(jnp.concatenate([token_ids, seg_lengths, counted], axis=1))

    ids_all = packed[:, :, :span].reshape(dp, tokens)
    piece_all = ids_all // vocab_rows
    local_all = ids_all % vocab_rows
    block_all = local_all // rows_unit
    hit = block_all[:, :, None] == jnp.arange(e_units)[None, None, :]
    slot_all = jnp.sum(jnp.where(hit, lay_e.slot[None, None, :], 0), axis=-1)
    code_all = piece_all * dp + slot_all // slots
    code_all = spread_f.step(spread_a.step(code_all))
    order = jnp.arange(tokens)
    earlier = order[None, None, :] < order[None, :, None]
    repeat = jnp.any((ids_all[:, :, None] == ids_all[:, None, :]) & earlier, axis=-1)
    first_all = ~repeat
    first_all = spread_e.step(first_all)
    rank_all = jnp.sum(
        (code_all[:, :, None] == code_all[:, None, :]) & earlier & first_all[:, None, :],
        axis=-1,
    ).astype(jnp.int32)
    rank_all = spread_f.step(spread_a.step(rank_all))
    rounds = jnp.max(jnp.where(first_all, rank_all, 0)) // PICK + 1
    mine_all = first_all & (code_all == piece * dp + me)
    row_all = (slot_all % slots) * rows_unit + local_all % rows_unit
    ids_own = token_ids.reshape(tokens)

    def own_view(array, which=me):
        return lax.dynamic_index_in_dim(array, which, 0, False)

    code_own = own_view(code_all)
    same = (ids_own[:, None] == ids_own[None, :]) & own_view(first_all)[None, :]
    rank_own = jnp.sum(jnp.where(same, own_view(rank_all)[None, :], 0), axis=-1)
    inside_own = (code_own // dp) == piece
    owner_own = code_own % dp

    def owner_picks(turn):
        wanted = turn * PICK + jnp.arange(PICK)
        hit = mine_all[:, None, :] & (rank_all[:, None, :] == wanted[None, :, None])
        row = jnp.sum(jnp.where(hit, row_all[:, None, :] + 1, 0), axis=-1) - 1
        row = row.reshape(dp * PICK)
        return (row[:, None] == jnp.arange(slots * rows_unit)[None, :]).astype(BF16)

    def token_picks(turn):
        rank = rank_own - turn * PICK
        good = inside_own & (rank >= 0) & (rank < PICK)
        key = jnp.where(good, owner_own * PICK + rank, -1)
        return (key[:, None] == jnp.arange(dp * PICK)[None, :]).astype(BF16)

    def find(turn):
        rows = dot_plain(owner_picks(turn), own.reshape(slots * rows_unit, width)).astype(BF16)
        return lax.all_to_all(rows.reshape(dp, PICK, width), "dp", 0, 0)

    def fill_in(turn, rows):
        return dot_plain(token_picks(turn), rows.reshape(dp * PICK, width)).astype(BF16)

    x0 = fill_in(0, find(0))
    x0 = lax.fori_loop(1, rounds, lambda i, t: t + fill_in(i, find(i)), x0)
    x0 = spread_e.step(x0)
    x0 = mp_sum(x0, True)
    x0 = spread_a.land(x0)
    swap_a = Swap(spread_a.finish(), lay_a, 13, 1)
    x0 = swap_a.launch(x0)
    x0 = spread_f.land(x0)
    swap_f = Swap(spread_f.finish(), lay_f, 26, 1)
    x0 = swap_f.launch(x0).astype(F32) * root

    gains = norm_params
    seg = segment_ids(seg_lengths, span)
    a1b = layer_norm(x0, gains[0], gains[1]).astype(BF16)
    a1b = swap_a.land(a1b)
    w_a = swap_a.finish()[lay_a.position].reshape(a_units * rows_unit, width)
    w_qkv, w_out = w_a[: 3 * q_rows], w_a[3 * q_rows :]
    qkv = dot_t(a1b, w_qkv).astype(BF16).reshape(packs, span, 3, heads, HD)
    qkv = spread_e.step(qkv)
    query, keys, values = qkv[:, :, 0], qkv[:, :, 1], qkv[:, :, 2]
    probs = attention_probs(query, keys, seg)
    mixed = jnp.einsum("bhqk,bkhd->bqhd", probs.astype(BF16), values, preferred_element_type=F32)
    mixed = mixed.reshape(tokens, heads * HD).astype(BF16)

    def stop_f(got):
        got = swap_f.land(got)
        later["f"] = swap_f.finish()[lay_f.position].reshape(f_units * rows_unit, width)
        return got

    later = {}
    x1 = x0 + mp_sum(dot_plain(mixed, w_out), False, (None, stop_f))
    w_up, w_down = later["f"][:ff_rows], later["f"][ff_rows:]
    x1 = spread_e.land(x1)
    table = spread_e.finish().reshape(usual * rows_unit, width)
    a2b = layer_norm(x1, gains[2], gains[3]).astype(BF16)
    pre = dot_t(a2b, w_up)
    hidden = jax.nn.gelu(pre).astype(BF16)
    x2 = x1 + mp_sum(dot_plain(hidden, w_down))
    final_low = layer_norm(x2, gains[4], gains[5]).astype(BF16)

    core = piece % 2
    theirs = dp_pair(half_of(final_low, core))
    theirs = in_order(theirs, mp_flip(theirs, 1), core)
    both = jnp.concatenate([final_low, theirs], axis=0)
    pair_data = jnp.stack([own_view(packed), own_view(packed, me ^ 1)])
    pair_ids = pair_data[:, :, :span]
    pair_lengths = pair_data[:, :, span : span + seg_lengths.shape[1]]
    pair_seg = segment_ids(pair_lengths.reshape(2 * packs, -1), span).reshape(2, packs, span)
    pair_counted = pair_data[:, :, span + seg_lengths.shape[1] :]
    counts = (pair_seg[:, :, 1:] == pair_seg[:, :, :-1]) & (pair_counted[:, :, :-1] == 1)
    keep = jnp.concatenate([counts, jnp.zeros((2, packs, 1), bool)], axis=2)
    keep = keep.astype(F32).reshape(2 * tokens)
    target = jnp.concatenate([pair_ids[:, :, 1:], pair_ids[:, :, :1]], axis=2)
    target = target.reshape(2 * tokens)
    t_local = target % vocab_rows
    here = (lay_e.col == me % 2)[None, :] & (
        (t_local // rows_unit)[:, None] == jnp.arange(e_units)[None, :]
    )
    t_block = jnp.sum(jnp.where(here, lay_e.position[None, :] + 1, 0), axis=1) - 1
    t_row = t_block * rows_unit + t_local % rows_unit
    t_row = jnp.where((target // vocab_rows == piece) & (t_block >= 0), t_row, -1)

    def scores(table, lay, low, both):
        place = jnp.arange(table.shape[0])
        real = (place < lay.high * rows_unit)[None, :]
        onehot = (place + low * rows_unit)[None, :] == t_row[:, None]
        return dot_t(both, table), real, onehot

    def measures(logits, real, onehot):
        top = jnp.max(jnp.where(real, logits, NEG_FILL), axis=-1)
        total = jnp.sum(jnp.where(real, jnp.exp(logits - top[:, None]), 0.0), axis=-1)
        picked = jnp.sum(jnp.where(onehot, logits, 0.0), axis=-1)
        return jnp.stack([top, total, picked])

    def slopes(logits, real, onehot, lse):
        prob = jnp.where(real, jnp.exp(logits - lse[:, None]), 0.0)
        return (keep[:, None] * (prob - onehot.astype(F32))).astype(BF16)

    logits, real, onehot = scores(table, lay_m, 0, both)
    stats = measures(logits, real, onehot)
    if lay_t is not None:

        def spill(own):
            stream = Spread(own[lay_t.local_at(most - usual)], lay_t, 8, 0)
            return stream.store.reshape(-1, width)

        def more_stats(stats, own, both):
            return merge_stats(stats, measures(*scores(spill(own), lay_t, usual, both)))

        stats = when(crowded, more_stats, stats, own, both)
    for bit in bits_of("mp"):
        stats = merge_stats(stats, mp_flip(stats, bit))
    their_stats = dp_pair(stats)
    their_stats = jnp.concatenate([their_stats[:, tokens:], their_stats[:, :tokens]], axis=1)
    stats = merge_stats(stats, their_stats)
    lse = stats[0] + jnp.log(stats[1])
    loss_sum = jnp.sum((keep * (lse - stats[2]))[:tokens])
    loss_count = jnp.sum(keep[:tokens])
    d_logits = slopes(logits, real, onehot, lse)
    half = tokens // 2

    def halved(total):
        total = total.reshape(2, tokens, width)
        sent = lax.dynamic_slice_in_dim(total, (1 - core) * half, half, 1)
        kept = lax.dynamic_slice_in_dim(total, core * half, half, 1)
        return kept, sent

    part, sent = halved(dot_plain(d_logits, table))
    d_logits, sent = together(d_logits, sent)
    swapped = mp_flip(sent, 1)
    grad_e = dot_first(d_logits, both).reshape(usual, rows_unit, width)
    part = part + swapped
    collect_e = Collect(grad_e, lay_m, 21, 4)
    collect_e.launch()
    part = part[0] + dp_pair(part[1].astype(BF16)).astype(F32)
    if lay_t is not None:

        def more_final(total, own, both, lse):
            rest = spill(own)
            slope = slopes(*scores(rest, lay_t, usual, both), lse)
            kept, sent = halved(dot_plain(slope, rest))
            kept = kept + mp_flip(sent, 1)
            return total + kept[0] + dp_pair(kept[1].astype(BF16)).astype(F32)

        part = part + when(crowded, more_final, jnp.zeros(part.shape, F32), own, both, lse)
    for bit in bits_of("mp")[1:]:
        part = rounded(part)
        part = part + collect_e.step(mp_flip(part.astype(BF16), bit)).astype(F32)
    d_final = in_order(part, mp_flip(part, 1), core)

    dx2, d_gf, d_bf = jax.vjp(layer_norm, x2, gains[4], gains[5])[1](d_final)
    dz = dx2.astype(BF16)
    d_hidden = dot_t(dz, w_down)
    d_pre = jax.vjp(jax.nn.gelu, pre)[1](d_hidden)[0].astype(BF16)

    def blocks_in_order(lay, parts):
        grad = jnp.concatenate(parts, axis=0).reshape(lay.count, rows_unit, width)
        return grad[lay.unit_at()]

    d_a2 = mp_sum(dot_plain(d_pre, w_up), False, (None, collect_e.step))
    grad_f = blocks_in_order(lay_f, [dot_first(d_pre, a2b), dot_first(hidden, dz)])
    fold_f = Fold(grad_f, lay_f, 26, 1)
    d_a2 = fold_f.launch(d_a2)
    dx1_norm, d_g2, d_b2 = jax.vjp(layer_norm, x1, gains[2], gains[3])[1](d_a2)
    dx1 = dx2 + dx1_norm
    dy = dx1.astype(BF16)
    d_mixed = dot_t(dy, w_out).astype(BF16).reshape(packs, span, heads, HD)
    d_probs = jnp.einsum("bqhd,bkhd->bhqk", d_mixed, values, preferred_element_type=F32)
    d_values = jnp.einsum(
        "bhqk,bqhd->bkhd", probs.astype(BF16), d_mixed, preferred_element_type=F32
    )
    d_probs = collect_e.step(d_probs)
    d_scores = (probs * (d_probs - jnp.sum(probs * d_probs, axis=-1, keepdims=True))).astype(BF16)
    d_query = jnp.einsum("bhqk,bkhd->bqhd", d_scores, keys, preferred_element_type=F32)
    d_keys = jnp.einsum("bhqk,bqhd->bkhd", d_scores, query, preferred_element_type=F32)
    d_query, d_keys = d_query * HD ** (-0.5), d_keys * HD ** (-0.5)
    d_qkv = jnp.stack([d_query, d_keys, d_values], axis=2)
    d_qkv = d_qkv.reshape(tokens, 3 * heads * HD).astype(BF16)

    d_a1 = dot_plain(d_qkv, w_qkv)
    grad_a = blocks_in_order(lay_a, [dot_first(d_qkv, a1b), dot_first(mixed, dy)])
    fold_a = Fold(grad_a, lay_a, 13, 1)
    fold_a.launch()

    def stop_e(got):
        got = fold_f.land(collect_e.land(got))
        later["f"] = Collect(fold_f.finish(), lay_f, 9, 3)
        return later["f"].launch(got)

    d_a1 = mp_sum(d_a1, False, (stop_e, None, lambda got: later["f"].step(got)))
    grad_e, collect_f = collect_e.finish(), later["f"]
    d_a1 = fold_a.land(d_a1)
    collect_a = Collect(fold_a.finish(), lay_a, 5, 3)
    d_a1 = collect_a.launch(d_a1)
    dx0_norm, d_g1, d_b1 = jax.vjp(layer_norm, x0, gains[0], gains[1])[1](d_a1)
    dx0 = dx1 + dx0_norm
    d_rows = dx0 * root
    d_high = rounded(d_rows)
    d_low = (d_rows - d_high).astype(BF16)
    d_high = d_high.astype(BF16)

    def give(turn):
        picks = token_picks(turn)
        rows = (dot_first(picks, d_high) + dot_first(picks, d_low)).astype(BF16)
        return lax.all_to_all(rows.reshape(dp, PICK, width), "dp", 0, 0)

    def take(turn, rows):
        return dot_first(owner_picks(turn), rows.reshape(dp * PICK, width))

    rows = collect_a.step(collect_f.step(give(0)))
    owned = take(0, rows)
    owned = lax.fori_loop(1, rounds, lambda i, t: t + take(i, give(i)), owned)
    owned = owned.reshape(slots, rows_unit, width)
    owned = collect_a.step(owned)
    if lay_t is not None:

        def more_owned(owned, own, both, lse):
            grad = dot_first(slopes(*scores(spill(own), lay_t, usual, both), lse), both)
            stream = Collect(grad.reshape(-1, rows_unit, width), lay_t, 8, 0)
            stream.rest()
            index = lay_t.at_slot(slots)
            block = stream.store[jnp.maximum(index, 0)]
            return owned + jnp.where((index >= 0)[:, None, None], block, 0.0)

        owned = when(crowded, more_owned, owned, own, both, lse)
    owned = collect_a.land(collect_f.land(owned))
    grad_f, grad_a = collect_f.finish(), collect_a.finish()
    index = [lay.at_slot(slots) for lay in (lay_m, lay_f, lay_a)]
    owned, squares = assemble(owned, (grad_e, grad_f, grad_a), index)

    owner_squares = small_sum(jnp.sum(squares), ("mp",))
    sums = jnp.stack([loss_sum, loss_count, owner_squares] + [jnp.zeros(())] * (width - 3))
    sums = small_sum(jnp.stack([d_g1, d_b1, d_g2, d_b2, d_gf, d_bf, sums, sums]), ("dp",))
    gain_grads, loss_sum, loss_count, owner_squares = sums[:6], sums[6, 0], sums[6, 1], sums[6, 2]
    clip_norm = jnp.sqrt(owner_squares + jnp.sum(gain_grads * gain_grads))
    factor = jnp.minimum(1.0, CLIP_LIMIT / (clip_norm + 1e-06))
    new_master, new_first, new_second = adam_update(
        master, factor * owned, first_moment, second_moment, WEIGHT_DECAY
    )
    new_norms, new_norm_first, new_norm_second = adam_update(
        norm_params, factor * gain_grads, norm_first, norm_second, 0.0
    )
    return (
        new_master,
        new_first,
        new_second,
        new_norms,
        new_norm_first,
        new_norm_second,
        clip_norm,
        loss_sum,
        loss_count,
    )


def solution(mesh):
    placed = (
        P("dp", None),
        P("dp", None),
        P("dp", None),
        P(),
        P("dp", "mp", None),
        P("dp", "mp", None),
        P("dp", "mp", None),
        P(),
        P(),
        P(),
    )
    return jax.shard_map(
        per_device,
        mesh=mesh,
        in_specs=placed,
        out_specs=(
            P("dp", "mp", None),
            P("dp", "mp", None),
            P("dp", "mp", None),
            P(),
            P(),
            P(),
            P(),
            P(),
            P(),
        ),
        check_vma=False,
    )
```

```python
import jax
import jax.numpy as jnp
from jax import lax
from jax.experimental import pallas as pl
from jax.experimental.layout import Layout as Order
from jax.experimental.layout import with_layout_constraint
from jax.experimental.pallas import tpu as pltpu
from jax.sharding import PartitionSpec as P

HEADS = 20
HD = 56
FF = 4480
V = 42112
STEP = 10


NORM_EPS = 1e-05
LEARN_RATE = 0.1
BETA_ONE = 0.9
BETA_TWO = 0.95
ADAM_EPS = 1e-08
WEIGHT_DECAY = 0.1
CLIP_LIMIT = 1.0
NEG_FILL = -1e30

PICK = 64
F32 = jnp.float32
BF16 = jnp.bfloat16


def dp_pair(value):
    size = lax.axis_size("dp")
    return lax.ppermute(value, "dp", [(d, d ^ 1) for d in range(size)])


def line_hop(value, lane):
    dp, mp = lax.axis_size("dp"), lax.axis_size("mp")
    moves = []
    for d in range(dp):
        for m in range(mp):
            to = d + 2 if (m + lane) % 2 == 0 else d - 2
            if 0 <= to < dp:
                moves.append((d * mp + m, to * mp + m))
    return lax.ppermute(value, ("dp", "mp"), moves)


def dp_flip(value, bit):
    size = lax.axis_size("dp")
    return lax.ppermute(value, "dp", [(d, d ^ bit) for d in range(size)])


def mp_flip(value, bit):
    size = lax.axis_size("mp")
    return lax.ppermute(value, "mp", [(d, d ^ bit) for d in range(size)])


def bits_of(axis):
    return [1 << k for k in range(lax.axis_size(axis).bit_length() - 1)]


def rounded(value):
    return lax.reduce_precision(value, 8, 7)


def half_of(value, which):
    count = value.shape[0] // 2
    return lax.dynamic_slice_in_dim(value, which * count, count, 0)


def in_order(mine, other, which):
    first = jnp.where(which == 0, mine, other)
    second = jnp.where(which == 0, other, mine)
    return jnp.concatenate([first, second], axis=0)


def mp_sum(value, exact=False, stops=()):
    stops = list(stops) + [None] * 3

    def hop(sent, bit, stop):
        got = mp_flip(sent, bit)
        return got if stop is None else stop(got)

    core = lax.axis_index("mp") % 2
    total = half_of(value, core)
    other = half_of(value, 1 - core)
    total = total + hop(other, 1, stops[0])
    for bit in bits_of("mp")[1:]:
        if exact:
            total = total + hop(total, bit, stops[1])
        else:
            total = rounded(total)
            total = total + hop(total.astype(BF16), bit, stops[1]).astype(F32)
    return in_order(total, hop(total, 1, stops[2]), core)


def small_sum(value, axes):
    for axis in axes:
        flip = mp_flip if axis == "mp" else dp_flip
        for bit in bits_of(axis):
            value = value + flip(value, bit)
    return value


def small_gather(value):
    value = value[None]
    me = lax.axis_index("dp")
    for bit in bits_of("dp"):
        value = in_order(value, dp_flip(value, bit), (me // bit) % 2)
    return value


def together(*values):
    return lax.optimization_barrier(values)


def ceil_div(a, b):
    return -((-a) // b)


class Layout:
    def __init__(self, slot, slots, per_line):
        owner = slot // slots
        line = lax.axis_size("dp") // 2
        row, col = owner // 2, owner % 2
        key = (col * line + row) * slots + slot % slots
        me = lax.axis_index("dp")
        rows = jnp.arange(line)
        on_line = (col[:, None] == jnp.arange(2)[None, :])[:, :, None]
        before = on_line & (row[:, None] < rows[None, :])[:, None, :]
        upto = on_line & (row[:, None] <= rows[None, :])[:, None, :]
        self.starts = jnp.sum(before, axis=0).astype(jnp.int32)
        self.ends = jnp.sum(upto, axis=0).astype(jnp.int32)
        self.total = self.ends[:, -1]
        self.base = jnp.zeros((2,), jnp.int32)
        position = jnp.sum(key[None, :] < key[:, None], axis=1).astype(jnp.int32)
        if per_line:
            position = position - jnp.where(col == 1, self.total[0], 0)
        else:
            self.base = self.total[0] * jnp.arange(2)
        self.position, self.col, self.local = position, col, slot % slots
        self.slot, self.count = slot, slot.shape[0]
        self.mine = owner == me
        self.place()

    def place(self):
        me = lax.axis_index("dp")
        z, x = me // 2, me % 2
        self.low, self.other_low = self.base[x], self.base[1 - x]
        self.high, self.other_high = self.low + self.total[x], self.other_low + self.total[1 - x]
        self.first, self.last = self.low + self.starts[x, z], self.low + self.ends[x, z]
        self.longest = jnp.max(self.total)

    def part(self, low, room):
        cut = object.__new__(Layout)
        cut.__dict__.update(self.__dict__)
        cut.starts = jnp.clip(self.starts - low, 0, room)
        cut.ends = jnp.clip(self.ends - low, 0, room)
        cut.total = jnp.clip(self.total - low, 0, room)
        inside = (self.position >= low) & (self.position < low + room)
        cut.position = jnp.where(inside, self.position - low, -1)
        cut.place()
        return cut

    def steps(self, chunk):
        rows = jnp.arange(self.starts.shape[1])
        last = self.starts.shape[1] - 1
        right = ceil_div(self.ends, chunk) + (last - 1 - rows)[None, :]
        left = ceil_div(self.total[:, None] - self.starts, chunk) + (rows - 1)[None, :]
        return jnp.maximum(jnp.max(right[:, :last]), jnp.max(left[:, 1:])).astype(jnp.int32)

    def local_at(self, places):
        hit = (self.position[None, :] == jnp.arange(places)[:, None]) & self.mine[None, :]
        return jnp.sum(jnp.where(hit, self.local[None, :], 0), axis=1)

    def unit_at(self):
        hit = self.position[None, :] == jnp.arange(self.count)[:, None]
        return jnp.sum(jnp.where(hit, jnp.arange(self.count)[None, :], 0), axis=1)

    def at_slot(self, slots):
        hit = self.mine[None, :] & (self.local[None, :] == jnp.arange(slots)[:, None])
        return jnp.sum(jnp.where(hit, self.position[None, :] + 1, 0), axis=1) - 1


def window(store, low, chunk):
    start = jnp.clip(low, 0, store.shape[0] - chunk)
    return start, lax.dynamic_slice_in_dim(store, start, chunk, 0)


def put(store, block, low, valid_low, valid_high, add):
    chunk = block.shape[0]
    start, old = window(store, low, chunk)
    least = jnp.maximum(low, valid_low) - start
    limit = jnp.minimum(low + chunk, valid_high) - start
    place = lax.broadcasted_iota(jnp.int32, block.shape, 0)
    good = (place >= least) & (place < limit)
    if add:
        new = old.astype(F32) + jnp.where(good, block.astype(F32), 0.0)
        new = new.astype(old.dtype)
    else:
        new = jnp.where(good, block, old)
    return lax.dynamic_update_slice_in_dim(store, new, start, 0)


class Stream:
    lanes = 1

    def __init__(self, store, lay, chunk, planned):
        self.store, self.lay, self.chunk, self.planned = store, lay, chunk, planned
        self.needed = jnp.where(lay.longest > 0, self.count_steps(), 0)
        self.done = 0
        self.flight = [None] * self.lanes
        self.prepare()

    def prepare(self):
        pass

    def one(self, store, k):
        blocks = [self.send(self.outgoing(store, k, n), n) for n in range(self.lanes)]
        for n in range(self.lanes):
            store = self.receive(store, blocks[n], k, n)
        return store

    def fly(self, lane, k, value):
        out = self.outgoing(self.store, k, lane)
        self.flight[lane] = self.send(out, lane)
        return value

    def fetch(self, lane, value):
        block = self.flight[lane]
        self.store = self.receive(self.store, block, self.k, lane)
        return value

    def launch(self, value=None):
        self.k = self.order(self.done)
        self.done += 1
        for lane in range(self.lanes):
            value = self.fly(lane, self.k, value)
        return value

    def land(self, value=None):
        for lane in range(self.lanes):
            value = self.fetch(lane, value)
        return value

    def step(self, value=None):
        k = self.order(self.done)
        self.done += 1
        for lane in range(self.lanes):
            value = self.fetch(lane, value)
            value = self.fly(lane, k, value)
        self.k = k
        return value

    def finish(self):
        assert self.done == self.planned
        self.rest()
        return self.store

    def order(self, n):
        return n

    def rest(self):
        self.store = lax.fori_loop(
            self.planned,
            jnp.maximum(self.needed, self.planned),
            lambda k, store: self.one(store, k),
            self.store,
        )


class LineStream(Stream):
    lanes = 2

    def count_steps(self):
        return self.lay.steps(self.chunk)

    def edges(self, k, lane):
        line = lax.axis_size("dp") // 2
        z = lax.axis_index("dp") // 2
        up = (lax.axis_index("mp") + lane) % 2 == 0
        lay, chunk = self.lay, self.chunk
        up_near = lay.low + (k - (line - 2 - z)) * chunk
        down_near = lay.high - (k - z + 2) * chunk
        near = jnp.where(up, up_near, down_near)
        return near, jnp.where(up, up_near - chunk, down_near + chunk), up


class Spread(LineStream):
    def prepare(self):
        self.store = lax.fori_loop(
            0,
            jnp.maximum(self.needed - self.planned, 0),
            lambda i, store: self.one(store, self.needed - 1 - i),
            self.store,
        )

    def order(self, n):
        return self.planned - 1 - n

    def rest(self):
        pass

    def outgoing(self, store, k, lane):
        return window(store, self.edges(k, lane)[0], self.chunk)[1]

    def send(self, out, lane):
        return line_hop(out, lane)

    def receive(self, store, block, k, lane):
        _, far, up = self.edges(k, lane)
        low = jnp.where(up, self.lay.low, self.lay.last)
        high = jnp.where(up, self.lay.first, self.lay.high)
        return put(store, block, far, low, high, False)


class Collect(LineStream):
    def outgoing(self, store, k, lane):
        return window(store, self.edges(k, lane)[1], self.chunk)[1].astype(BF16)

    def send(self, out, lane):
        return line_hop(out, 1 - lane)

    def receive(self, store, block, k, lane):
        near, _, up = self.edges(k, lane)
        low = jnp.where(up, self.lay.low, self.lay.first)
        high = jnp.where(up, self.lay.last, self.lay.high)
        return put(store, block, near, low, high, True)


class PairStream(Stream):
    def count_steps(self):
        return ceil_div(self.lay.longest, self.chunk)

    def send(self, out, lane):
        return dp_pair(out)


class Swap(PairStream):
    def outgoing(self, store, k, lane):
        return window(store, self.lay.low + k * self.chunk, self.chunk)[1]

    def receive(self, store, block, k, lane):
        lay = self.lay
        low = lay.other_low + k * self.chunk
        return put(store, block, low, lay.other_low, lay.other_high, False)


class Fold(PairStream):
    def outgoing(self, store, k, lane):
        low = self.lay.other_low + k * self.chunk
        return window(store, low, self.chunk)[1].astype(BF16)

    def receive(self, store, block, k, lane):
        lay = self.lay
        return put(store, block, lay.low + k * self.chunk, lay.low, lay.high, True)


def layer_norm(x, gain, shift):
    centred = x - jnp.mean(x, axis=-1, keepdims=True)
    scale = lax.rsqrt(jnp.mean(centred * centred, axis=-1, keepdims=True) + NORM_EPS)
    return centred * scale * gain + shift


def segment_ids(lengths, span):
    bounds = jnp.cumsum(lengths, axis=-1)
    return jnp.sum(jnp.arange(span)[None, :, None] >= bounds[:, None, :], axis=-1)


def dot_t(left, right):
    return lax.dot_general(left, right, (((1,), (1,)), ((), ())), preferred_element_type=F32)


def dot_first(left, right):
    return lax.dot_general(left, right, (((0,), (0,)), ((), ())), preferred_element_type=F32)


def dot_plain(left, right):
    return jnp.dot(left, right, preferred_element_type=F32)


def attention_probs(query, keys, seg):
    span = seg.shape[1]
    scores = jnp.einsum("bqhd,bkhd->bhqk", query, keys, preferred_element_type=F32) * HD ** (-0.5)
    place = jnp.arange(span)
    allowed = (seg[:, :, None] == seg[:, None, :]) & (place[None, None, :] <= place[None, :, None])
    scores = jnp.where(allowed[:, None], scores, NEG_FILL)
    expo = jnp.exp(scores - jnp.max(scores, axis=-1, keepdims=True))
    return expo / jnp.sum(expo, axis=-1, keepdims=True)


def assemble_kernel(kind_ref, e_at, f_at, a_at, rows_ref, e_ref, f_ref, a_ref, out_ref, sq_ref):
    slot = pl.program_id(0)
    kind = kind_ref[slot]
    value = jnp.where(kind == 0, e_ref[...].astype(F32), 0.0)
    value = jnp.where(kind == 1, f_ref[...], value)
    value = rows_ref[...] + jnp.where(kind == 2, a_ref[...], value)
    out_ref[...] = value

    @pl.when(slot == 0)
    def _():
        sq_ref[...] = jnp.zeros(sq_ref.shape, F32)

    _, rows, width = value.shape
    sq_ref[...] += jnp.sum((value * value).reshape(rows // 8, 8, width), axis=0)


def assemble(rows, grads, index):
    slots, rows_unit, width = rows.shape
    kind = jnp.full((slots,), 3, jnp.int32)
    for number, at in enumerate(index):
        kind = jnp.where(at >= 0, number, kind)
    places = jnp.arange(slots)

    def held(at):
        used = jnp.where((at >= 0)[None, :] & (places[None, :] <= places[:, None]), places, -1)
        latest = jnp.max(used, axis=1)
        same = places[None, :] == latest[:, None]
        return jnp.sum(jnp.where(same, at[None, :], 0), axis=1).astype(jnp.int32)

    index = [held(at) for at in index]
    block = (1, rows_unit, width)
    return pl.pallas_call(
        assemble_kernel,
        grid_spec=pltpu.PrefetchScalarGridSpec(
            num_scalar_prefetch=4,
            grid=(slots,),
            in_specs=[
                pl.BlockSpec(block, lambda s, k, e, f, a: (s, 0, 0)),
                pl.BlockSpec(block, lambda s, k, e, f, a: (e[s], 0, 0)),
                pl.BlockSpec(block, lambda s, k, e, f, a: (f[s], 0, 0)),
                pl.BlockSpec(block, lambda s, k, e, f, a: (a[s], 0, 0)),
            ],
            out_specs=[
                pl.BlockSpec(block, lambda s, k, e, f, a: (s, 0, 0)),
                pl.BlockSpec((8, width), lambda s, k, e, f, a: (0, 0)),
            ],
        ),
        out_shape=[
            jax.ShapeDtypeStruct(rows.shape, F32),
            jax.ShapeDtypeStruct((8, width), F32),
        ],
    )(kind, *index, rows, *grads)


def when(wanted, work, value, *given):
    def turn(i, so_far):
        i, *held = together(i, *given)
        return work(so_far, *held)

    return lax.fori_loop(0, wanted.astype(jnp.int32), turn, value)


def adam_update(weight, grad, first, second, decay):
    first = BETA_ONE * first + (1.0 - BETA_ONE) * grad
    second = BETA_TWO * second + (1.0 - BETA_TWO) * grad * grad
    stride = first / (1.0 - BETA_ONE**STEP) / (jnp.sqrt(second / (1.0 - BETA_TWO**STEP)) + ADAM_EPS)
    return (weight - LEARN_RATE * (stride + decay * weight), first, second)


def merge_stats(left, right):
    top = jnp.maximum(left[0], right[0])
    total = left[1] * jnp.exp(left[0] - top) + right[1] * jnp.exp(right[0] - top)
    return jnp.stack([top, total, left[2] + right[2]])


def per_device(
    token_ids,
    seg_lengths,
    counted,
    unit_slot,
    master,
    first_moment,
    second_moment,
    norm_params,
    norm_first,
    norm_second,
):
    slots, rows_unit, width = master.shape
    dp = lax.axis_size("dp")
    parts = lax.axis_size("mp")
    me = lax.axis_index("dp")
    piece = lax.axis_index("mp")
    heads = HEADS // parts
    q_rows = heads * HD
    ff_rows = FF // parts
    vocab_rows = V // parts
    a_units = 4 * q_rows // rows_unit
    f_units = 2 * ff_rows // rows_unit
    e_units = vocab_rows // rows_unit
    packs, span = token_ids.shape
    tokens = packs * span
    root = width**0.5
    line = dp // 2

    a_end, f_end = a_units, a_units + f_units
    lay_a = Layout(unit_slot[:a_end], slots, False)
    lay_f = Layout(unit_slot[a_end:f_end], slots, False)
    lay_e = Layout(unit_slot[f_end:], slots, True)
    most = min(e_units, line * slots)
    usual = min(most, 112)
    crowded = lay_e.longest > usual
    lay_m = lay_e.part(0, usual)
    lay_t = lay_e.part(usual, most - usual) if most > usual else None

    own = master.astype(BF16)

    at_a, at_f, at_e = lay_a.local_at(a_units), lay_f.local_at(f_units), lay_m.local_at(usual)
    spread_a = Spread(master[at_a].astype(BF16), lay_a, 5, 3)
    at_f = spread_a.launch(at_f)
    spread_f = Spread(own[at_f], lay_f, 9, 3)
    at_e = spread_f.launch(at_e)
    spread_e = Spread(own[at_e], lay_m, 21, 4)
    spread_e.launch()
    packed = small_gather(jnp.concatenate([token_ids, seg_lengths, counted], axis=1))

    ids_all = packed[:, :, :span].reshape(dp, tokens)
    piece_all = ids_all // vocab_rows
    local_all = ids_all % vocab_rows
    block_all = local_all // rows_unit
    hit = block_all[:, :, None] == jnp.arange(e_units)[None, None, :]
    slot_all = jnp.sum(jnp.where(hit, lay_e.slot[None, None, :], 0), axis=-1)
    code_all = piece_all * dp + slot_all // slots
    code_all = spread_f.step(spread_a.step(code_all))
    order = jnp.arange(tokens)
    earlier = order[None, None, :] < order[None, :, None]
    repeat = jnp.any((ids_all[:, :, None] == ids_all[:, None, :]) & earlier, axis=-1)
    first_all = ~repeat
    first_all = spread_e.step(first_all)
    rank_all = jnp.sum(
        (code_all[:, :, None] == code_all[:, None, :]) & earlier & first_all[:, None, :],
        axis=-1,
    ).astype(jnp.int32)
    rank_all = spread_f.step(spread_a.step(rank_all))
    rounds = jnp.max(jnp.where(first_all, rank_all, 0)) // PICK + 1
    mine_all = first_all & (code_all == piece * dp + me)
    row_all = (slot_all % slots) * rows_unit + local_all % rows_unit
    ids_own = token_ids.reshape(tokens)

    def own_view(array, which=me):
        return lax.dynamic_index_in_dim(array, which, 0, False)

    code_own = own_view(code_all)
    same = (ids_own[:, None] == ids_own[None, :]) & own_view(first_all)[None, :]
    rank_own = jnp.sum(jnp.where(same, own_view(rank_all)[None, :], 0), axis=-1)
    inside_own = (code_own // dp) == piece
    owner_own = code_own % dp

    def owner_picks(turn):
        wanted = turn * PICK + jnp.arange(PICK)
        hit = mine_all[:, None, :] & (rank_all[:, None, :] == wanted[None, :, None])
        row = jnp.sum(jnp.where(hit, row_all[:, None, :] + 1, 0), axis=-1) - 1
        row = row.reshape(dp * PICK)
        return (row[:, None] == jnp.arange(slots * rows_unit)[None, :]).astype(BF16)

    def token_picks(turn):
        rank = rank_own - turn * PICK
        good = inside_own & (rank >= 0) & (rank < PICK)
        key = jnp.where(good, owner_own * PICK + rank, -1)
        return (key[:, None] == jnp.arange(dp * PICK)[None, :]).astype(BF16)

    def find(turn):
        rows = dot_plain(owner_picks(turn), own.reshape(slots * rows_unit, width)).astype(BF16)
        return lax.all_to_all(rows.reshape(dp, PICK, width), "dp", 0, 0)

    def fill_in(turn, rows):
        return dot_plain(token_picks(turn), rows.reshape(dp * PICK, width)).astype(BF16)

    x0 = fill_in(0, find(0))
    x0 = lax.fori_loop(1, rounds, lambda i, t: t + fill_in(i, find(i)), x0)
    x0 = spread_e.step(x0)
    x0 = mp_sum(x0, True)
    x0 = spread_a.land(x0)
    swap_a = Swap(spread_a.finish(), lay_a, 13, 1)
    x0 = swap_a.launch(x0)
    x0 = spread_f.land(x0)
    swap_f = Swap(spread_f.finish(), lay_f, 26, 1)
    x0 = swap_f.launch(x0).astype(F32) * root

    gains = norm_params
    seg = segment_ids(seg_lengths, span)
    a1b = layer_norm(x0, gains[0], gains[1]).astype(BF16)
    a1b = swap_a.land(a1b)
    w_a = swap_a.finish()[lay_a.position].reshape(a_units * rows_unit, width)
    w_qkv, w_out = w_a[: 3 * q_rows], w_a[3 * q_rows :]
    qkv = dot_t(a1b, w_qkv).astype(BF16).reshape(packs, span, 3, heads, HD)
    qkv = spread_e.step(qkv)
    query, keys, values = qkv[:, :, 0], qkv[:, :, 1], qkv[:, :, 2]
    probs = attention_probs(query, keys, seg)
    mixed = jnp.einsum("bhqk,bkhd->bqhd", probs.astype(BF16), values, preferred_element_type=F32)
    mixed = mixed.reshape(tokens, heads * HD).astype(BF16)

    def stop_f(got):
        got = swap_f.land(got)
        later["f"] = swap_f.finish()[lay_f.position].reshape(f_units * rows_unit, width)
        return got

    later = {}
    x1 = x0 + mp_sum(dot_plain(mixed, w_out), False, (None, stop_f))
    w_up, w_down = later["f"][:ff_rows], later["f"][ff_rows:]
    x1 = spread_e.land(x1)
    table = spread_e.finish().reshape(usual * rows_unit, width)
    a2b = layer_norm(x1, gains[2], gains[3]).astype(BF16)
    pre = dot_t(a2b, w_up)
    hidden = jax.nn.gelu(pre).astype(BF16)
    x2 = x1 + mp_sum(dot_plain(hidden, w_down))
    final_low = layer_norm(x2, gains[4], gains[5]).astype(BF16)

    core = piece % 2
    theirs = dp_pair(half_of(final_low, core))
    theirs = in_order(theirs, mp_flip(theirs, 1), core)
    both = jnp.concatenate([final_low, theirs], axis=0)
    pair_data = jnp.stack([own_view(packed), own_view(packed, me ^ 1)])
    pair_ids = pair_data[:, :, :span]
    pair_lengths = pair_data[:, :, span : span + seg_lengths.shape[1]]
    pair_seg = segment_ids(pair_lengths.reshape(2 * packs, -1), span).reshape(2, packs, span)
    pair_counted = pair_data[:, :, span + seg_lengths.shape[1] :]
    counts = (pair_seg[:, :, 1:] == pair_seg[:, :, :-1]) & (pair_counted[:, :, :-1] == 1)
    keep = jnp.concatenate([counts, jnp.zeros((2, packs, 1), bool)], axis=2)
    keep = keep.astype(F32).reshape(2 * tokens)
    target = jnp.concatenate([pair_ids[:, :, 1:], pair_ids[:, :, :1]], axis=2)
    target = target.reshape(2 * tokens)
    t_local = target % vocab_rows
    here = (lay_e.col == me % 2)[None, :] & (
        (t_local // rows_unit)[:, None] == jnp.arange(e_units)[None, :]
    )
    t_block = jnp.sum(jnp.where(here, lay_e.position[None, :] + 1, 0), axis=1) - 1
    t_row = t_block * rows_unit + t_local % rows_unit
    t_row = jnp.where((target // vocab_rows == piece) & (t_block >= 0), t_row, -1)

    def scores(table, lay, low, both):
        place = jnp.arange(table.shape[0])
        real = (place < lay.high * rows_unit)[None, :]
        onehot = (place + low * rows_unit)[None, :] == t_row[:, None]
        return dot_t(both, table), real, onehot

    def measures(logits, real, onehot):
        top = jnp.max(jnp.where(real, logits, NEG_FILL), axis=-1)
        total = jnp.sum(jnp.where(real, jnp.exp(logits - top[:, None]), 0.0), axis=-1)
        picked = jnp.sum(jnp.where(onehot, logits, 0.0), axis=-1)
        return jnp.stack([top, total, picked])

    def slopes(logits, real, onehot, lse):
        prob = jnp.where(real, jnp.exp(logits - lse[:, None]), 0.0)
        return (keep[:, None] * (prob - onehot.astype(F32))).astype(BF16)

    logits, real, onehot = scores(table, lay_m, 0, both)
    stats = measures(logits, real, onehot)
    if lay_t is not None:

        def spill(own):
            stream = Spread(own[lay_t.local_at(most - usual)], lay_t, 8, 0)
            return stream.store.reshape(-1, width)

        def more_stats(stats, own, both):
            return merge_stats(stats, measures(*scores(spill(own), lay_t, usual, both)))

        stats = when(crowded, more_stats, stats, own, both)
    for bit in bits_of("mp"):
        stats = merge_stats(stats, mp_flip(stats, bit))
    their_stats = dp_pair(stats)
    their_stats = jnp.concatenate([their_stats[:, tokens:], their_stats[:, :tokens]], axis=1)
    stats = merge_stats(stats, their_stats)
    lse = stats[0] + jnp.log(stats[1])
    loss_sum = jnp.sum((keep * (lse - stats[2]))[:tokens])
    loss_count = jnp.sum(keep[:tokens])
    d_logits = slopes(logits, real, onehot, lse)
    half = tokens // 2

    def halved(total):
        total = total.reshape(2, tokens, width)
        sent = lax.dynamic_slice_in_dim(total, (1 - core) * half, half, 1)
        kept = lax.dynamic_slice_in_dim(total, core * half, half, 1)
        return kept, sent

    part, sent = halved(dot_plain(d_logits, table))
    d_logits, sent = together(d_logits, sent)
    swapped = mp_flip(sent, 1)
    grad_e = with_layout_constraint(dot_first(d_logits, both), Order((0, 1))).astype(BF16)
    grad_e = grad_e.reshape(usual, rows_unit, width)
    part = part + swapped
    collect_e = Collect(grad_e, lay_m, 21, 4)
    collect_e.launch()
    part = part[0] + dp_pair(part[1].astype(BF16)).astype(F32)
    if lay_t is not None:

        def more_final(total, own, both, lse):
            rest = spill(own)
            slope = slopes(*scores(rest, lay_t, usual, both), lse)
            kept, sent = halved(dot_plain(slope, rest))
            kept = kept + mp_flip(sent, 1)
            return total + kept[0] + dp_pair(kept[1].astype(BF16)).astype(F32)

        part = part + when(crowded, more_final, jnp.zeros(part.shape, F32), own, both, lse)
    for bit in bits_of("mp")[1:]:
        part = rounded(part)
        part = part + collect_e.step(mp_flip(part.astype(BF16), bit)).astype(F32)
    d_final = in_order(part, mp_flip(part, 1), core)

    dx2, d_gf, d_bf = jax.vjp(layer_norm, x2, gains[4], gains[5])[1](d_final)
    dz = dx2.astype(BF16)
    d_hidden = dot_t(dz, w_down)
    d_pre = jax.vjp(jax.nn.gelu, pre)[1](d_hidden)[0].astype(BF16)

    def blocks_in_order(lay, parts):
        grad = jnp.concatenate(parts, axis=0).reshape(lay.count, rows_unit, width)
        return grad[lay.unit_at()]

    d_a2 = mp_sum(dot_plain(d_pre, w_up), False, (None, collect_e.step))
    grad_f = blocks_in_order(lay_f, [dot_first(d_pre, a2b), dot_first(hidden, dz)])
    fold_f = Fold(grad_f, lay_f, 26, 1)
    d_a2 = fold_f.launch(d_a2)
    dx1_norm, d_g2, d_b2 = jax.vjp(layer_norm, x1, gains[2], gains[3])[1](d_a2)
    dx1 = dx2 + dx1_norm
    dy = dx1.astype(BF16)
    d_mixed = dot_t(dy, w_out).astype(BF16).reshape(packs, span, heads, HD)
    d_probs = jnp.einsum("bqhd,bkhd->bhqk", d_mixed, values, preferred_element_type=F32)
    d_values = jnp.einsum(
        "bhqk,bqhd->bkhd", probs.astype(BF16), d_mixed, preferred_element_type=F32
    )
    d_probs = collect_e.step(d_probs)
    d_scores = (probs * (d_probs - jnp.sum(probs * d_probs, axis=-1, keepdims=True))).astype(BF16)
    d_query = jnp.einsum("bhqk,bkhd->bqhd", d_scores, keys, preferred_element_type=F32)
    d_keys = jnp.einsum("bhqk,bqhd->bkhd", d_scores, query, preferred_element_type=F32)
    d_query, d_keys = d_query * HD ** (-0.5), d_keys * HD ** (-0.5)
    d_qkv = jnp.stack([d_query, d_keys, d_values], axis=2)
    d_qkv = d_qkv.reshape(tokens, 3 * heads * HD).astype(BF16)

    d_a1 = dot_plain(d_qkv, w_qkv)
    grad_a = blocks_in_order(lay_a, [dot_first(d_qkv, a1b), dot_first(mixed, dy)])
    fold_a = Fold(grad_a, lay_a, 13, 1)
    fold_a.launch()

    def stop_e(got):
        got = fold_f.land(collect_e.land(got))
        later["f"] = Collect(fold_f.finish(), lay_f, 9, 3)
        return later["f"].launch(got)

    d_a1 = mp_sum(d_a1, False, (stop_e, None, lambda got: later["f"].step(got)))
    grad_e, collect_f = collect_e.finish(), later["f"]
    d_a1 = fold_a.land(d_a1)
    collect_a = Collect(fold_a.finish(), lay_a, 5, 3)
    d_a1 = collect_a.launch(d_a1)
    dx0_norm, d_g1, d_b1 = jax.vjp(layer_norm, x0, gains[0], gains[1])[1](d_a1)
    dx0 = dx1 + dx0_norm
    d_rows = dx0 * root
    d_high = rounded(d_rows)
    d_low = (d_rows - d_high).astype(BF16)
    d_high = d_high.astype(BF16)

    def give(turn):
        picks = token_picks(turn)
        rows = (dot_first(picks, d_high) + dot_first(picks, d_low)).astype(BF16)
        return lax.all_to_all(rows.reshape(dp, PICK, width), "dp", 0, 0)

    def take(turn, rows):
        return dot_first(owner_picks(turn), rows.reshape(dp * PICK, width))

    collect_f.step()
    collect_a.step()
    collect_a.step()
    collect_f.land()
    collect_a.land()

    def more_owned(owned, own, both, lse):
        grad = dot_first(slopes(*scores(spill(own), lay_t, usual, both), lse), both)
        stream = Collect(grad.reshape(-1, rows_unit, width), lay_t, 8, 0)
        stream.rest()
        index = lay_t.at_slot(slots)
        block = stream.store[jnp.maximum(index, 0)]
        block = jnp.where((index >= 0)[:, None, None], block, 0.0)
        return owned + block.reshape(owned.shape)

    def more(i, owned):
        if lay_t is None:
            return owned + take(i, give(i))
        j, *held = together(i, own, both, lse)
        return lax.cond(
            j < rounds,
            lambda: owned + take(j, give(j)),
            lambda: more_owned(owned, *held),
        )

    turns = rounds if lay_t is None else rounds + crowded.astype(jnp.int32)
    owned = lax.fori_loop(1, turns, more, take(0, give(0)))
    owned = owned.reshape(slots, rows_unit, width)
    grad_f, grad_a = collect_f.finish(), collect_a.finish()
    index = [lay.at_slot(slots) for lay in (lay_m, lay_f, lay_a)]
    owned, squares = assemble(owned, (grad_e, grad_f, grad_a), index)

    owner_squares = small_sum(jnp.sum(squares), ("mp",))
    sums = jnp.stack([loss_sum, loss_count, owner_squares] + [jnp.zeros(())] * (width - 3))
    sums = small_sum(jnp.stack([d_g1, d_b1, d_g2, d_b2, d_gf, d_bf, sums, sums]), ("dp",))
    gain_grads, loss_sum, loss_count, owner_squares = sums[:6], sums[6, 0], sums[6, 1], sums[6, 2]
    clip_norm = jnp.sqrt(owner_squares + jnp.sum(gain_grads * gain_grads))
    factor = jnp.minimum(1.0, CLIP_LIMIT / (clip_norm + 1e-06))
    new_master, new_first, new_second = adam_update(
        master, factor * owned, first_moment, second_moment, WEIGHT_DECAY
    )
    new_norms, new_norm_first, new_norm_second = adam_update(
        norm_params, factor * gain_grads, norm_first, norm_second, 0.0
    )
    return (
        new_master,
        new_first,
        new_second,
        new_norms,
        new_norm_first,
        new_norm_second,
        clip_norm,
        loss_sum,
        loss_count,
    )


def solution(mesh):
    placed = (
        P("dp", None),
        P("dp", None),
        P("dp", None),
        P(),
        P("dp", "mp", None),
        P("dp", "mp", None),
        P("dp", "mp", None),
        P(),
        P(),
        P(),
    )
    return jax.shard_map(
        per_device,
        mesh=mesh,
        in_specs=placed,
        out_specs=(
            P("dp", "mp", None),
            P("dp", "mp", None),
            P("dp", "mp", None),
            P(),
            P(),
            P(),
            P(),
            P(),
            P(),
        ),
        check_vma=False,
    )
```

```python
import jax
import jax.numpy as jnp
from jax import lax
from jax.experimental import pallas as pl
from jax.experimental.layout import Layout as Order
from jax.experimental.layout import with_layout_constraint
from jax.experimental.pallas import tpu as pltpu
from jax.sharding import PartitionSpec as P

HEADS = 20
HD = 56
FF = 4480
V = 42112
STEP = 10


NORM_EPS = 1e-05
LEARN_RATE = 0.1
BETA_ONE = 0.9
BETA_TWO = 0.95
ADAM_EPS = 1e-08
WEIGHT_DECAY = 0.1
CLIP_LIMIT = 1.0
NEG_FILL = -1e30

PICK = 48
F32 = jnp.float32
BF16 = jnp.bfloat16


def dp_pair(value):
    size = lax.axis_size("dp")
    return lax.ppermute(value, "dp", [(d, d ^ 1) for d in range(size)])


def line_hop(value, lane):
    dp, mp = lax.axis_size("dp"), lax.axis_size("mp")
    moves = []
    for d in range(dp):
        for m in range(mp):
            to = d + 2 if (m + lane) % 2 == 0 else d - 2
            if 0 <= to < dp:
                moves.append((d * mp + m, to * mp + m))
    return lax.ppermute(value, ("dp", "mp"), moves)


def dp_flip(value, bit):
    size = lax.axis_size("dp")
    return lax.ppermute(value, "dp", [(d, d ^ bit) for d in range(size)])


def mp_flip(value, bit):
    size = lax.axis_size("mp")
    return lax.ppermute(value, "mp", [(d, d ^ bit) for d in range(size)])


def bits_of(axis):
    return [1 << k for k in range(lax.axis_size(axis).bit_length() - 1)]


def rounded(value):
    return lax.reduce_precision(value, 8, 7)


def half_of(value, which):
    count = value.shape[0] // 2
    return lax.dynamic_slice_in_dim(value, which * count, count, 0)


def in_order(mine, other, which):
    first = jnp.where(which == 0, mine, other)
    second = jnp.where(which == 0, other, mine)
    return jnp.concatenate([first, second], axis=0)


def mp_sum(value, exact=False, stops=()):
    stops = list(stops) + [None] * 3

    def hop(sent, bit, stop):
        got = mp_flip(sent, bit)
        return got if stop is None else stop(got)

    core = lax.axis_index("mp") % 2
    total = half_of(value, core)
    other = half_of(value, 1 - core)
    total = total + hop(other, 1, stops[0])
    for bit in bits_of("mp")[1:]:
        if exact:
            total = total + hop(total, bit, stops[1])
        else:
            total = rounded(total)
            total = total + hop(total.astype(BF16), bit, stops[1]).astype(F32)
    return in_order(total, hop(total, 1, stops[2]), core)


def small_sum(value, axes):
    for axis in axes:
        flip = mp_flip if axis == "mp" else dp_flip
        for bit in bits_of(axis):
            value = value + flip(value, bit)
    return value


def small_gather(value):
    value = value[None]
    me = lax.axis_index("dp")
    for bit in bits_of("dp"):
        value = in_order(value, dp_flip(value, bit), (me // bit) % 2)
    return value


def together(*values):
    return lax.optimization_barrier(values)


def ceil_div(a, b):
    return -((-a) // b)


class Layout:
    def __init__(self, slot, slots, per_line):
        owner = slot // slots
        line = lax.axis_size("dp") // 2
        row, col = owner // 2, owner % 2
        key = (col * line + row) * slots + slot % slots
        me = lax.axis_index("dp")
        rows = jnp.arange(line)
        on_line = (col[:, None] == jnp.arange(2)[None, :])[:, :, None]
        before = on_line & (row[:, None] < rows[None, :])[:, None, :]
        upto = on_line & (row[:, None] <= rows[None, :])[:, None, :]
        self.starts = jnp.sum(before, axis=0).astype(jnp.int32)
        self.ends = jnp.sum(upto, axis=0).astype(jnp.int32)
        self.total = self.ends[:, -1]
        self.base = jnp.zeros((2,), jnp.int32)
        position = jnp.sum(key[None, :] < key[:, None], axis=1).astype(jnp.int32)
        if per_line:
            position = position - jnp.where(col == 1, self.total[0], 0)
        else:
            self.base = self.total[0] * jnp.arange(2)
        self.position, self.col, self.local = position, col, slot % slots
        self.slot, self.count = slot, slot.shape[0]
        self.mine = owner == me
        self.place()

    def place(self):
        me = lax.axis_index("dp")
        z, x = me // 2, me % 2
        self.low, self.other_low = self.base[x], self.base[1 - x]
        self.high, self.other_high = self.low + self.total[x], self.other_low + self.total[1 - x]
        self.first, self.last = self.low + self.starts[x, z], self.low + self.ends[x, z]
        self.longest = jnp.max(self.total)

    def part(self, low, room):
        cut = object.__new__(Layout)
        cut.__dict__.update(self.__dict__)
        cut.starts = jnp.clip(self.starts - low, 0, room)
        cut.ends = jnp.clip(self.ends - low, 0, room)
        cut.total = jnp.clip(self.total - low, 0, room)
        inside = (self.position >= low) & (self.position < low + room)
        cut.position = jnp.where(inside, self.position - low, -1)
        cut.place()
        return cut

    def steps(self, chunk):
        rows = jnp.arange(self.starts.shape[1])
        last = self.starts.shape[1] - 1
        right = ceil_div(self.ends, chunk) + (last - 1 - rows)[None, :]
        left = ceil_div(self.total[:, None] - self.starts, chunk) + (rows - 1)[None, :]
        return jnp.maximum(jnp.max(right[:, :last]), jnp.max(left[:, 1:])).astype(jnp.int32)

    def local_at(self, places):
        hit = (self.position[None, :] == jnp.arange(places)[:, None]) & self.mine[None, :]
        return jnp.sum(jnp.where(hit, self.local[None, :], 0), axis=1)

    def unit_at(self):
        hit = self.position[None, :] == jnp.arange(self.count)[:, None]
        return jnp.sum(jnp.where(hit, jnp.arange(self.count)[None, :], 0), axis=1)

    def at_slot(self, slots):
        hit = self.mine[None, :] & (self.local[None, :] == jnp.arange(slots)[:, None])
        return jnp.sum(jnp.where(hit, self.position[None, :] + 1, 0), axis=1) - 1


def window(store, low, chunk):
    start = jnp.clip(low, 0, store.shape[0] - chunk)
    return start, lax.dynamic_slice_in_dim(store, start, chunk, 0)


def put(store, block, low, valid_low, valid_high, add):
    chunk = block.shape[0]
    start, old = window(store, low, chunk)
    least = jnp.maximum(low, valid_low) - start
    limit = jnp.minimum(low + chunk, valid_high) - start
    place = lax.broadcasted_iota(jnp.int32, block.shape, 0)
    good = (place >= least) & (place < limit)
    if add:
        new = old.astype(F32) + jnp.where(good, block.astype(F32), 0.0)
        new = new.astype(old.dtype)
    else:
        new = jnp.where(good, block, old)
    return lax.dynamic_update_slice_in_dim(store, new, start, 0)


class Stream:
    lanes = 1

    def __init__(self, store, lay, chunk, planned):
        self.store, self.lay, self.chunk, self.planned = store, lay, chunk, planned
        self.needed = jnp.where(lay.longest > 0, self.count_steps(), 0)
        self.done = 0
        self.flight = [None] * self.lanes
        self.prepare()

    def prepare(self):
        pass

    def one(self, store, k):
        blocks = [self.send(self.outgoing(store, k, n), n) for n in range(self.lanes)]
        for n in range(self.lanes):
            store = self.receive(store, blocks[n], k, n)
        return store

    def fly(self, lane, k, value):
        out = self.outgoing(self.store, k, lane)
        self.flight[lane] = self.send(out, lane)
        return value

    def fetch(self, lane, value):
        block = self.flight[lane]
        self.store = self.receive(self.store, block, self.k, lane)
        return value

    def launch(self, value=None):
        self.k = self.order(self.done)
        self.done += 1
        for lane in range(self.lanes):
            value = self.fly(lane, self.k, value)
        return value

    def land(self, value=None):
        for lane in range(self.lanes):
            value = self.fetch(lane, value)
        return value

    def step(self, value=None):
        k = self.order(self.done)
        self.done += 1
        for lane in range(self.lanes):
            value = self.fetch(lane, value)
            value = self.fly(lane, k, value)
        self.k = k
        return value

    def finish(self):
        assert self.done == self.planned
        self.rest()
        return self.store

    def order(self, n):
        return n

    def rest(self):
        self.store = lax.fori_loop(
            self.planned,
            jnp.maximum(self.needed, self.planned),
            lambda k, store: self.one(store, k),
            self.store,
        )


class LineStream(Stream):
    lanes = 2

    def count_steps(self):
        return self.lay.steps(self.chunk)

    def edges(self, k, lane):
        line = lax.axis_size("dp") // 2
        z = lax.axis_index("dp") // 2
        up = (lax.axis_index("mp") + lane) % 2 == 0
        lay, chunk = self.lay, self.chunk
        up_near = lay.low + (k - (line - 2 - z)) * chunk
        down_near = lay.high - (k - z + 2) * chunk
        near = jnp.where(up, up_near, down_near)
        return near, jnp.where(up, up_near - chunk, down_near + chunk), up


class Spread(LineStream):
    def prepare(self):
        self.store = lax.fori_loop(
            0,
            jnp.maximum(self.needed - self.planned, 0),
            lambda i, store: self.one(store, self.needed - 1 - i),
            self.store,
        )

    def order(self, n):
        return self.planned - 1 - n

    def rest(self):
        pass

    def outgoing(self, store, k, lane):
        return window(store, self.edges(k, lane)[0], self.chunk)[1]

    def send(self, out, lane):
        return line_hop(out, lane)

    def receive(self, store, block, k, lane):
        _, far, up = self.edges(k, lane)
        low = jnp.where(up, self.lay.low, self.lay.last)
        high = jnp.where(up, self.lay.first, self.lay.high)
        return put(store, block, far, low, high, False)


class Collect(LineStream):
    def outgoing(self, store, k, lane):
        return window(store, self.edges(k, lane)[1], self.chunk)[1].astype(BF16)

    def send(self, out, lane):
        return line_hop(out, 1 - lane)

    def receive(self, store, block, k, lane):
        near, _, up = self.edges(k, lane)
        low = jnp.where(up, self.lay.low, self.lay.first)
        high = jnp.where(up, self.lay.last, self.lay.high)
        return put(store, block, near, low, high, True)


class PairStream(Stream):
    def count_steps(self):
        return ceil_div(self.lay.longest, self.chunk)

    def send(self, out, lane):
        return dp_pair(out)


class Swap(PairStream):
    def outgoing(self, store, k, lane):
        return window(store, self.lay.low + k * self.chunk, self.chunk)[1]

    def receive(self, store, block, k, lane):
        lay = self.lay
        low = lay.other_low + k * self.chunk
        return put(store, block, low, lay.other_low, lay.other_high, False)


class Fold(PairStream):
    def outgoing(self, store, k, lane):
        low = self.lay.other_low + k * self.chunk
        return window(store, low, self.chunk)[1].astype(BF16)

    def receive(self, store, block, k, lane):
        lay = self.lay
        return put(store, block, lay.low + k * self.chunk, lay.low, lay.high, True)


def layer_norm(x, gain, shift):
    centred = x - jnp.mean(x, axis=-1, keepdims=True)
    scale = lax.rsqrt(jnp.mean(centred * centred, axis=-1, keepdims=True) + NORM_EPS)
    return centred * scale * gain + shift


def segment_ids(lengths, span):
    bounds = jnp.cumsum(lengths, axis=-1)
    return jnp.sum(jnp.arange(span)[None, :, None] >= bounds[:, None, :], axis=-1)


def dot_t(left, right):
    return lax.dot_general(left, right, (((1,), (1,)), ((), ())), preferred_element_type=F32)


def dot_first(left, right):
    return lax.dot_general(left, right, (((0,), (0,)), ((), ())), preferred_element_type=F32)


def dot_plain(left, right):
    return jnp.dot(left, right, preferred_element_type=F32)


def attention_probs(query, keys, seg):
    span = seg.shape[1]
    scores = jnp.einsum("bqhd,bkhd->bhqk", query, keys, preferred_element_type=F32) * HD ** (-0.5)
    place = jnp.arange(span)
    allowed = (seg[:, :, None] == seg[:, None, :]) & (place[None, None, :] <= place[None, :, None])
    scores = jnp.where(allowed[:, None], scores, NEG_FILL)
    expo = jnp.exp(scores - jnp.max(scores, axis=-1, keepdims=True))
    return expo / jnp.sum(expo, axis=-1, keepdims=True)


def assemble_kernel(kind_ref, e_at, f_at, a_at, rows_ref, e_ref, f_ref, a_ref, out_ref, sq_ref):
    slot = pl.program_id(0)
    kind = kind_ref[slot]
    value = jnp.where(kind == 0, e_ref[...].astype(F32), 0.0)
    value = jnp.where(kind == 1, f_ref[...], value)
    value = rows_ref[...] + jnp.where(kind == 2, a_ref[...], value)
    out_ref[...] = value

    @pl.when(slot == 0)
    def _():
        sq_ref[...] = jnp.zeros(sq_ref.shape, F32)

    _, rows, width = value.shape
    sq_ref[...] += jnp.sum((value * value).reshape(rows // 8, 8, width), axis=0)


def assemble(rows, grads, index):
    slots, rows_unit, width = rows.shape
    kind = jnp.full((slots,), 3, jnp.int32)
    for number, at in enumerate(index):
        kind = jnp.where(at >= 0, number, kind)
    places = jnp.arange(slots)

    def held(at):
        used = jnp.where((at >= 0)[None, :] & (places[None, :] <= places[:, None]), places, -1)
        latest = jnp.max(used, axis=1)
        same = places[None, :] == latest[:, None]
        return jnp.sum(jnp.where(same, at[None, :], 0), axis=1).astype(jnp.int32)

    index = [held(at) for at in index]
    block = (1, rows_unit, width)
    return pl.pallas_call(
        assemble_kernel,
        grid_spec=pltpu.PrefetchScalarGridSpec(
            num_scalar_prefetch=4,
            grid=(slots,),
            in_specs=[
                pl.BlockSpec(block, lambda s, k, e, f, a: (s, 0, 0)),
                pl.BlockSpec(block, lambda s, k, e, f, a: (e[s], 0, 0)),
                pl.BlockSpec(block, lambda s, k, e, f, a: (f[s], 0, 0)),
                pl.BlockSpec(block, lambda s, k, e, f, a: (a[s], 0, 0)),
            ],
            out_specs=[
                pl.BlockSpec(block, lambda s, k, e, f, a: (s, 0, 0)),
                pl.BlockSpec((8, width), lambda s, k, e, f, a: (0, 0)),
            ],
        ),
        out_shape=[
            jax.ShapeDtypeStruct(rows.shape, F32),
            jax.ShapeDtypeStruct((8, width), F32),
        ],
    )(kind, *index, rows, *grads)


def when(wanted, work, value, *given):
    def turn(i, so_far):
        i, *held = together(i, *given)
        return work(so_far, *held)

    return lax.fori_loop(0, wanted.astype(jnp.int32), turn, value)


def adam_update(weight, grad, first, second, decay):
    first = BETA_ONE * first + (1.0 - BETA_ONE) * grad
    second = BETA_TWO * second + (1.0 - BETA_TWO) * grad * grad
    stride = first / (1.0 - BETA_ONE**STEP) / (jnp.sqrt(second / (1.0 - BETA_TWO**STEP)) + ADAM_EPS)
    return (weight - LEARN_RATE * (stride + decay * weight), first, second)


def merge_stats(left, right):
    top = jnp.maximum(left[0], right[0])
    total = left[1] * jnp.exp(left[0] - top) + right[1] * jnp.exp(right[0] - top)
    return jnp.stack([top, total, left[2] + right[2]])


def per_device(
    token_ids,
    seg_lengths,
    counted,
    unit_slot,
    master,
    first_moment,
    second_moment,
    norm_params,
    norm_first,
    norm_second,
):
    slots, rows_unit, width = master.shape
    dp = lax.axis_size("dp")
    parts = lax.axis_size("mp")
    me = lax.axis_index("dp")
    piece = lax.axis_index("mp")
    heads = HEADS // parts
    q_rows = heads * HD
    ff_rows = FF // parts
    vocab_rows = V // parts
    a_units = 4 * q_rows // rows_unit
    f_units = 2 * ff_rows // rows_unit
    e_units = vocab_rows // rows_unit
    packs, span = token_ids.shape
    tokens = packs * span
    root = width**0.5
    line = dp // 2

    a_end, f_end = a_units, a_units + f_units
    lay_a = Layout(unit_slot[:a_end], slots, False)
    lay_f = Layout(unit_slot[a_end:f_end], slots, False)
    lay_e = Layout(unit_slot[f_end:], slots, True)
    most = min(e_units, line * slots)
    usual = min(most, 112)
    crowded = lay_e.longest > usual
    lay_m = lay_e.part(0, usual)
    lay_t = lay_e.part(usual, most - usual) if most > usual else None

    own = master.astype(BF16)

    at_a, at_f, at_e = lay_a.local_at(a_units), lay_f.local_at(f_units), lay_m.local_at(usual)
    spread_a = Spread(master[at_a].astype(BF16), lay_a, 5, 3)
    at_f = spread_a.launch(at_f)
    spread_f = Spread(own[at_f], lay_f, 9, 3)
    at_e = spread_f.launch(at_e)
    spread_e = Spread(own[at_e], lay_m, 21, 4)
    spread_e.launch()
    packed = small_gather(jnp.concatenate([token_ids, seg_lengths, counted], axis=1))

    ids_all = packed[:, :, :span].reshape(dp, tokens)
    piece_all = ids_all // vocab_rows
    local_all = ids_all % vocab_rows
    block_all = local_all // rows_unit
    hit = block_all[:, :, None] == jnp.arange(e_units)[None, None, :]
    slot_all = jnp.sum(jnp.where(hit, lay_e.slot[None, None, :], 0), axis=-1)
    code_all = piece_all * dp + slot_all // slots
    code_all = spread_f.step(spread_a.step(code_all))
    order = jnp.arange(tokens)
    earlier = order[None, None, :] < order[None, :, None]
    repeat = jnp.any((ids_all[:, :, None] == ids_all[:, None, :]) & earlier, axis=-1)
    first_all = ~repeat
    first_all = spread_e.step(first_all)
    rank_all = jnp.sum(
        (code_all[:, :, None] == code_all[:, None, :]) & earlier & first_all[:, None, :],
        axis=-1,
    ).astype(jnp.int32)
    rank_all = spread_f.step(spread_a.step(rank_all))
    rounds = jnp.max(jnp.where(first_all, rank_all, 0)) // PICK + 1
    mine_all = first_all & (code_all == piece * dp + me)
    row_all = (slot_all % slots) * rows_unit + local_all % rows_unit
    ids_own = token_ids.reshape(tokens)

    def own_view(array, which=me):
        return lax.dynamic_index_in_dim(array, which, 0, False)

    code_own = own_view(code_all)
    same = (ids_own[:, None] == ids_own[None, :]) & own_view(first_all)[None, :]
    rank_own = jnp.sum(jnp.where(same, own_view(rank_all)[None, :], 0), axis=-1)
    inside_own = (code_own // dp) == piece
    owner_own = code_own % dp

    def owner_picks(turn):
        wanted = turn * PICK + jnp.arange(PICK)
        hit = mine_all[:, None, :] & (rank_all[:, None, :] == wanted[None, :, None])
        row = jnp.sum(jnp.where(hit, row_all[:, None, :] + 1, 0), axis=-1) - 1
        row = row.reshape(dp * PICK)
        return (row[:, None] == jnp.arange(slots * rows_unit)[None, :]).astype(BF16)

    def token_picks(turn):
        rank = rank_own - turn * PICK
        good = inside_own & (rank >= 0) & (rank < PICK)
        key = jnp.where(good, owner_own * PICK + rank, -1)
        return (key[:, None] == jnp.arange(dp * PICK)[None, :]).astype(BF16)

    def find(turn):
        rows = dot_plain(owner_picks(turn), own.reshape(slots * rows_unit, width)).astype(BF16)
        return lax.all_to_all(rows.reshape(dp, PICK, width), "dp", 0, 0)

    def fill_in(turn, rows):
        return dot_plain(token_picks(turn), rows.reshape(dp * PICK, width)).astype(BF16)

    x0 = fill_in(0, find(0))
    x0 = lax.fori_loop(1, rounds, lambda i, t: t + fill_in(i, find(i)), x0)
    x0 = spread_e.step(x0)
    x0 = mp_sum(x0, True)
    x0 = spread_a.land(x0)
    swap_a = Swap(spread_a.finish(), lay_a, 13, 1)
    x0 = swap_a.launch(x0)
    x0 = spread_f.land(x0)
    swap_f = Swap(spread_f.finish(), lay_f, 26, 1)
    x0 = swap_f.launch(x0).astype(F32) * root

    gains = norm_params
    seg = segment_ids(seg_lengths, span)
    a1b = layer_norm(x0, gains[0], gains[1]).astype(BF16)
    a1b = swap_a.land(a1b)
    w_a = swap_a.finish()[lay_a.position].reshape(a_units * rows_unit, width)
    w_qkv, w_out = w_a[: 3 * q_rows], w_a[3 * q_rows :]
    qkv = dot_t(a1b, w_qkv).astype(BF16).reshape(packs, span, 3, heads, HD)
    qkv = spread_e.step(qkv)
    query, keys, values = qkv[:, :, 0], qkv[:, :, 1], qkv[:, :, 2]
    probs = attention_probs(query, keys, seg)
    mixed = jnp.einsum("bhqk,bkhd->bqhd", probs.astype(BF16), values, preferred_element_type=F32)
    mixed = mixed.reshape(tokens, heads * HD).astype(BF16)

    def stop_f(got):
        got = swap_f.land(got)
        later["f"] = swap_f.finish()[lay_f.position].reshape(f_units * rows_unit, width)
        return got

    later = {}
    x1 = x0 + mp_sum(dot_plain(mixed, w_out), False, (None, stop_f))
    w_up, w_down = later["f"][:ff_rows], later["f"][ff_rows:]
    x1 = spread_e.land(x1)
    table = spread_e.finish().reshape(usual * rows_unit, width)
    a2b = layer_norm(x1, gains[2], gains[3]).astype(BF16)
    pre = dot_t(a2b, w_up)
    hidden = jax.nn.gelu(pre).astype(BF16)
    x2 = x1 + mp_sum(dot_plain(hidden, w_down))
    final_low = layer_norm(x2, gains[4], gains[5]).astype(BF16)

    core = piece % 2
    theirs = dp_pair(half_of(final_low, core))
    theirs = in_order(theirs, mp_flip(theirs, 1), core)
    both = jnp.concatenate([final_low, theirs], axis=0)
    pair_data = jnp.stack([own_view(packed), own_view(packed, me ^ 1)])
    pair_ids = pair_data[:, :, :span]
    pair_lengths = pair_data[:, :, span : span + seg_lengths.shape[1]]
    pair_seg = segment_ids(pair_lengths.reshape(2 * packs, -1), span).reshape(2, packs, span)
    pair_counted = pair_data[:, :, span + seg_lengths.shape[1] :]
    counts = (pair_seg[:, :, 1:] == pair_seg[:, :, :-1]) & (pair_counted[:, :, :-1] == 1)
    keep = jnp.concatenate([counts, jnp.zeros((2, packs, 1), bool)], axis=2)
    keep = keep.astype(F32).reshape(2 * tokens)
    target = jnp.concatenate([pair_ids[:, :, 1:], pair_ids[:, :, :1]], axis=2)
    target = target.reshape(2 * tokens)
    t_local = target % vocab_rows
    here = (lay_e.col == me % 2)[None, :] & (
        (t_local // rows_unit)[:, None] == jnp.arange(e_units)[None, :]
    )
    t_block = jnp.sum(jnp.where(here, lay_e.position[None, :] + 1, 0), axis=1) - 1
    t_row = t_block * rows_unit + t_local % rows_unit
    t_row = jnp.where((target // vocab_rows == piece) & (t_block >= 0), t_row, -1)

    def scores(table, lay, low, both):
        place = jnp.arange(table.shape[0])
        real = (place < lay.high * rows_unit)[None, :]
        onehot = (place + low * rows_unit)[None, :] == t_row[:, None]
        return dot_t(both, table), real, onehot

    def measures(logits, real, onehot):
        top = jnp.max(jnp.where(real, logits, NEG_FILL), axis=-1)
        total = jnp.sum(jnp.where(real, jnp.exp(logits - top[:, None]), 0.0), axis=-1)
        picked = jnp.sum(jnp.where(onehot, logits, 0.0), axis=-1)
        return jnp.stack([top, total, picked])

    def slopes(logits, real, onehot, lse):
        prob = jnp.where(real, jnp.exp(logits - lse[:, None]), 0.0)
        return (keep[:, None] * (prob - onehot.astype(F32))).astype(BF16)

    logits, real, onehot = scores(table, lay_m, 0, both)
    stats = measures(logits, real, onehot)
    if lay_t is not None:

        def spill(own):
            stream = Spread(own[lay_t.local_at(most - usual)], lay_t, 8, 0)
            return stream.store.reshape(-1, width)

        def more_stats(stats, own, both):
            return merge_stats(stats, measures(*scores(spill(own), lay_t, usual, both)))

        stats = when(crowded, more_stats, stats, own, both)
    for bit in bits_of("mp"):
        stats = merge_stats(stats, mp_flip(stats, bit))
    their_stats = dp_pair(stats)
    their_stats = jnp.concatenate([their_stats[:, tokens:], their_stats[:, :tokens]], axis=1)
    stats = merge_stats(stats, their_stats)
    lse = stats[0] + jnp.log(stats[1])
    loss_sum = jnp.sum((keep * (lse - stats[2]))[:tokens])
    loss_count = jnp.sum(keep[:tokens])
    d_logits = slopes(logits, real, onehot, lse)
    half = tokens // 2

    def halved(total):
        total = total.reshape(2, tokens, width)
        sent = lax.dynamic_slice_in_dim(total, (1 - core) * half, half, 1)
        kept = lax.dynamic_slice_in_dim(total, core * half, half, 1)
        return kept, sent

    part, sent = halved(dot_plain(d_logits, table))
    d_logits, sent = together(d_logits, sent)
    swapped = mp_flip(sent, 1)
    grad_e = with_layout_constraint(dot_first(d_logits, both), Order((0, 1))).astype(BF16)
    grad_e = grad_e.reshape(usual, rows_unit, width)
    part = part + swapped
    collect_e = Collect(grad_e, lay_m, 21, 4)
    collect_e.launch()
    part = part[0] + dp_pair(part[1].astype(BF16)).astype(F32)
    if lay_t is not None:

        def more_final(total, own, both, lse):
            rest = spill(own)
            slope = slopes(*scores(rest, lay_t, usual, both), lse)
            kept, sent = halved(dot_plain(slope, rest))
            kept = kept + mp_flip(sent, 1)
            return total + kept[0] + dp_pair(kept[1].astype(BF16)).astype(F32)

        part = part + when(crowded, more_final, jnp.zeros(part.shape, F32), own, both, lse)
    for bit in bits_of("mp")[1:]:
        part = rounded(part)
        part = part + collect_e.step(mp_flip(part.astype(BF16), bit)).astype(F32)
    d_final = in_order(part, mp_flip(part, 1), core)

    dx2, d_gf, d_bf = jax.vjp(layer_norm, x2, gains[4], gains[5])[1](d_final)
    dz = dx2.astype(BF16)
    d_hidden = dot_t(dz, w_down)
    d_pre = jax.vjp(jax.nn.gelu, pre)[1](d_hidden)[0].astype(BF16)

    def blocks_in_order(lay, parts):
        grad = jnp.concatenate(parts, axis=0).reshape(lay.count, rows_unit, width)
        return grad[lay.unit_at()]

    d_a2 = mp_sum(dot_plain(d_pre, w_up), False, (None, collect_e.step))
    grad_f = blocks_in_order(lay_f, [dot_first(d_pre, a2b), dot_first(hidden, dz)])
    fold_f = Fold(grad_f, lay_f, 26, 1)
    d_a2 = fold_f.launch(d_a2)
    dx1_norm, d_g2, d_b2 = jax.vjp(layer_norm, x1, gains[2], gains[3])[1](d_a2)
    dx1 = dx2 + dx1_norm
    dy = dx1.astype(BF16)
    d_mixed = dot_t(dy, w_out).astype(BF16).reshape(packs, span, heads, HD)
    d_probs = jnp.einsum("bqhd,bkhd->bhqk", d_mixed, values, preferred_element_type=F32)
    d_values = jnp.einsum(
        "bhqk,bqhd->bkhd", probs.astype(BF16), d_mixed, preferred_element_type=F32
    )
    d_probs = collect_e.step(d_probs)
    d_scores = (probs * (d_probs - jnp.sum(probs * d_probs, axis=-1, keepdims=True))).astype(BF16)
    d_query = jnp.einsum("bhqk,bkhd->bqhd", d_scores, keys, preferred_element_type=F32)
    d_keys = jnp.einsum("bhqk,bqhd->bkhd", d_scores, query, preferred_element_type=F32)
    d_query, d_keys = d_query * HD ** (-0.5), d_keys * HD ** (-0.5)
    d_qkv = jnp.stack([d_query, d_keys, d_values], axis=2)
    d_qkv = d_qkv.reshape(tokens, 3 * heads * HD).astype(BF16)

    d_a1 = dot_plain(d_qkv, w_qkv)
    grad_a = blocks_in_order(lay_a, [dot_first(d_qkv, a1b), dot_first(mixed, dy)])
    fold_a = Fold(grad_a, lay_a, 13, 1)
    fold_a.launch()

    def stop_e(got):
        got = fold_f.land(collect_e.land(got))
        later["f"] = Collect(fold_f.finish(), lay_f, 9, 3)
        return later["f"].launch(got)

    d_a1 = mp_sum(d_a1, False, (stop_e, None, lambda got: later["f"].step(got)))
    grad_e, collect_f = collect_e.finish(), later["f"]
    d_a1 = fold_a.land(d_a1)
    collect_a = Collect(fold_a.finish(), lay_a, 5, 3)
    d_a1 = collect_a.launch(d_a1)
    dx0_norm, d_g1, d_b1 = jax.vjp(layer_norm, x0, gains[0], gains[1])[1](d_a1)
    dx0 = dx1 + dx0_norm
    d_rows = dx0 * root
    d_high = rounded(d_rows)
    d_low = (d_rows - d_high).astype(BF16)
    d_high = d_high.astype(BF16)

    def give(turn):
        picks = token_picks(turn)
        rows = (dot_first(picks, d_high) + dot_first(picks, d_low)).astype(BF16)
        return lax.all_to_all(rows.reshape(dp, PICK, width), "dp", 0, 0)

    def take(turn, rows):
        return dot_first(owner_picks(turn), rows.reshape(dp * PICK, width))

    collect_f.step()
    collect_a.step()
    collect_a.step()
    collect_f.land()
    collect_a.land()

    def more_owned(owned, own, both, lse):
        grad = dot_first(slopes(*scores(spill(own), lay_t, usual, both), lse), both)
        stream = Collect(grad.reshape(-1, rows_unit, width), lay_t, 8, 0)
        stream.rest()
        index = lay_t.at_slot(slots)
        block = stream.store[jnp.maximum(index, 0)]
        block = jnp.where((index >= 0)[:, None, None], block, 0.0)
        return owned + block.reshape(owned.shape)

    def more(i, owned):
        if lay_t is None:
            return owned + take(i, give(i))
        j, *held = together(i, own, both, lse)
        return lax.cond(
            j < rounds,
            lambda: owned + take(j, give(j)),
            lambda: more_owned(owned, *held),
        )

    turns = rounds if lay_t is None else rounds + crowded.astype(jnp.int32)
    owned = lax.fori_loop(1, turns, more, take(0, give(0)))
    owned = owned.reshape(slots, rows_unit, width)
    grad_f, grad_a = collect_f.finish(), collect_a.finish()
    index = [lay.at_slot(slots) for lay in (lay_m, lay_f, lay_a)]
    owned, squares = assemble(owned, (grad_e, grad_f, grad_a), index)

    owner_squares = small_sum(jnp.sum(squares), ("mp",))
    sums = jnp.stack([loss_sum, loss_count, owner_squares] + [jnp.zeros(())] * (width - 3))
    sums = small_sum(jnp.stack([d_g1, d_b1, d_g2, d_b2, d_gf, d_bf, sums, sums]), ("dp",))
    gain_grads, loss_sum, loss_count, owner_squares = sums[:6], sums[6, 0], sums[6, 1], sums[6, 2]
    clip_norm = jnp.sqrt(owner_squares + jnp.sum(gain_grads * gain_grads))
    factor = jnp.minimum(1.0, CLIP_LIMIT / (clip_norm + 1e-06))
    new_master, new_first, new_second = adam_update(
        master, factor * owned, first_moment, second_moment, WEIGHT_DECAY
    )
    new_norms, new_norm_first, new_norm_second = adam_update(
        norm_params, factor * gain_grads, norm_first, norm_second, 0.0
    )
    return (
        new_master,
        new_first,
        new_second,
        new_norms,
        new_norm_first,
        new_norm_second,
        clip_norm,
        loss_sum,
        loss_count,
    )


def solution(mesh):
    placed = (
        P("dp", None),
        P("dp", None),
        P("dp", None),
        P(),
        P("dp", "mp", None),
        P("dp", "mp", None),
        P("dp", "mp", None),
        P(),
        P(),
        P(),
    )
    return jax.shard_map(
        per_device,
        mesh=mesh,
        in_specs=placed,
        out_specs=(
            P("dp", "mp", None),
            P("dp", "mp", None),
            P("dp", "mp", None),
            P(),
            P(),
            P(),
            P(),
            P(),
            P(),
        ),
        check_vma=False,
    )
```
